32 devices in a mesh: sub: 16 (over z, y, core), slab: 2 (over x).
Axes of the slice: x: 2, y: 2, z: 4, core: 2. Of those that a mesh axis runs over, the one named last changes fastest.
Arguments:
- source: float32 [4, 65536], P(None, ('sub', 'slab')), may hold values from -6 to 6
- operator: float32 [7, 4, 4, 65536], P(None, None, None, ('sub', 'slab')), as said below
- prolong: float32 [4, 4, 65536], P(None, None, ('sub', 'slab')), may hold values from -2 to 2
- columns: int32 [7, 65536], P(None, ('sub', 'slab')), may hold values from 0 to 4095, as said below
- slots: int32 [7, 65536], P(None, ('sub', 'slab')), may hold values from 0 to 6
- aggregates: int32 [65536], P(('sub', 'slab')), may hold values from 0 to 255, as said below
- sends: int32 [65536], P(('sub', 'slab')), may hold values from 0 to 2047, as said below
- prolong_one: float32 [4, 4, 16384], P(None, None, ('sub', 'slab')), as said below
- columns_one: int32 [7, 16384], P(None, ('sub', 'slab')), may hold values from 0 to 895, as said below
- slots_one: int32 [7, 16384], P(None, ('sub', 'slab')), may hold values from 0 to 6, as said below
- aggregates_one: int32 [16384], P(('sub', 'slab')), may hold values from 0 to 63, as said below
- sends_one: int32 [12288], P(('sub', 'slab')), may hold values from 0 to 511, as said below
- columns_two: int32 [7, 4096], P(None, ('sub', 'slab')), may hold values from 0 to 287, as said below
- sends_two: int32 [5120], P(('sub', 'slab')), may hold values from 0 to 127, as said below
Outputs:
- smoothed: float32 [4, 65536], P(None, ('sub', 'slab'))
- smoothed_one: float32 [4, 8192], P(None, ('sub', 'slab'))
- smoothed_two: float32 [4, 1024], P(None, ('sub', 'slab'))
The draws below stay inside these ranges and needn't reach their ends.
Inputs may be any that keep to these rules, and one draw needn't show every extreme that they name: Fine operator blocks; no other structure. `columns`: values below 2048 name the subdomain's own rows, the rest its ghost rows; every neighbour of a fine cell lies one or two cells away along one grid dimension, the third dimension closes into a loop. `aggregates`: eight fine rows a first-level aggregate. `sends`: local row numbers of the fine subdomain. `prolong_one`: equal on the two devices of a merged subdomain. `columns_one`: values below 512 name the merged subdomain's rows, the rest its ghost rows; equal on both devices of a merged subdomain. `slots_one`: equal on both devices of a merged subdomain. `aggregates_one`: eight first-level rows a second-level aggregate; equal on both devices of a merged subdomain. `sends_one`: row numbers of the merged first-level subdomain. `columns_two`: values below 128 name the merged subdomain's rows, the rest its ghost rows; equal on all four devices of a merged subdomain. `sends_two`: row numbers of the merged second-level subdomain.
All inputs are finite; a program needn't handle non-finite values.
Results may differ from the reference program's by a relative error of at most 0.0001.
Values sent between devices are 32-bit elements; how exact they have to be, the bound alone decides.
No kernel may reach another device: no remote copies, remote signals or barrier semaphores. Data moves between devices by JAX's collectives and lax.ppermute only.
A program may use at most 128 MiB of HBM per device.

```python
from functools import partial
import jax
import jax.numpy as jnp
from jax import lax

GX = 8
GY = 8
GZ = 32
CELLS = 2048
N_SUB = 16
N_SLAB = 2
DEVICES = 32


DIRECTIONS = ((0, 0, 0), (-1, 0, 0), (1, 0, 0), (0, -1, 0), (0, 1, 0), (0, 0, -1), (0, 0, 1))


def level_shape(level):
    return (GX >> level, GY, GZ >> level, N_SUB >> level)


def exchange_values(values, first, second):
    return jnp.where(values == first, second, jnp.where(values == second, first, values))


def level_numbering(key, level):
    span_x, span_y, span_z, groups = level_shape(level)
    halves = 1 if level == 0 else 2
    half_y = span_y // halves
    half_cells = span_x * half_y * span_z
    subkeys = jax.random.split(jax.random.fold_in(key, 100 + level), groups * N_SLAB * halves)

    def permute(subkey):
        order = jax.random.permutation(subkey, half_cells).astype(jnp.int32)
        order = exchange_values(order, order[0], jnp.int32(0))
        order = exchange_values(order, order[half_cells - 1], jnp.int32(half_cells - 1))
        return order
    perms = jax.vmap(permute)(subkeys)
    perms = perms.reshape(groups, N_SLAB, halves, span_x, half_y, span_z)
    perms = perms + (jnp.arange(halves, dtype=jnp.int32) * half_cells).reshape(1, 1, halves, 1, 1, 1)
    return perms.transpose(0, 1, 3, 2, 4, 5).reshape(groups, N_SLAB, span_x, span_y, span_z)


def level_coords(level):
    span_x, span_y, span_z, groups = level_shape(level)
    shape = (groups, N_SLAB, span_x, span_y, span_z)
    return [lax.broadcasted_iota(jnp.int32, shape, axis) for axis in range(5)]


def level_links(number, level, distance):
    span_x, span_y, span_z, groups = level_shape(level)
    depth = 2 if level == 0 else 1
    cells = span_x * span_y * span_z
    first_count = depth * span_y * span_z
    second_count = span_x * depth * span_z
    group_id, slab_id, coord_x, coord_y, coord_z = level_coords(level)
    result = []
    for slot_index in range(7):
        dir_x, dir_y, dir_z = DIRECTIONS[slot_index]
        stride = distance[slot_index]
        near_x = coord_x + dir_x * stride
        near_y = coord_y + dir_y * stride
        near_z = (coord_z + dir_z * stride) % span_z
        clip_x = jnp.clip(near_x, 0, span_x - 1)
        clip_y = jnp.clip(near_y, 0, span_y - 1)
        local = number[group_id, slab_id, clip_x, clip_y, near_z]
        below_x = cells + ((near_x + depth) * span_y + near_y) * span_z + near_z
        above_x = cells + first_count + ((near_x - span_x) * span_y + near_y) * span_z + near_z
        below_y = cells + 2 * first_count + (near_x * depth + near_y + depth) * span_z + near_z
        above_y = cells + 2 * first_count + second_count + (near_x * depth + near_y - span_y) * span_z + near_z
        link = jnp.where(near_x < 0, below_x, jnp.where(near_x >= span_x, above_x, jnp.where(near_y < 0, below_y, jnp.where(near_y >= span_y, above_y, local))))
        result.append(link.astype(jnp.int32))
    return jnp.stack(result)


def level_slots(level, distance):
    span_x, span_y, span_z, groups = level_shape(level)
    group_id, slab_id, coord_x, coord_y, coord_z = level_coords(level)
    result = []
    for slot_index in range(7):
        dir_x, dir_y, dir_z = DIRECTIONS[slot_index]
        stride = distance[slot_index]
        same = ((coord_x + dir_x * stride) // 2 == coord_x // 2) & ((coord_y + dir_y * stride) // 2 == coord_y // 2)
        same = same & ((coord_z + dir_z * stride) % span_z // 2 == coord_z // 2)
        result.append(jnp.where(same, 0, slot_index).astype(jnp.int32))
    return jnp.stack(result)


def level_aggregates(level, next_number):
    span_x, span_y, span_z, groups = level_shape(level)
    group_id, slab_id, coord_x, coord_y, coord_z = level_coords(level)
    coarse_global = (group_id * span_y + coord_y) // 2
    coarse_group = coarse_global // span_y
    coarse_y = coarse_global % span_y
    index = next_number[coarse_group, slab_id, coord_x // 2, coarse_y, coord_z // 2]
    half_cells = span_x // 2 * span_y * (span_z // 2) // 2
    return (index - (coarse_y >= span_y // 2).astype(jnp.int32) * half_cells).astype(jnp.int32)


def level_sends(number, level):
    span_x, span_y, span_z, groups = level_shape(level)
    depth = 2 if level == 0 else 1
    low_first = number[:, :, :depth].reshape(groups, N_SLAB, -1)
    high_first = number[:, :, span_x - depth:].reshape(groups, N_SLAB, -1)
    low_second = number[:, :, :, :depth].reshape(groups, N_SLAB, -1)
    high_second = number[:, :, :, span_y - depth:].reshape(groups, N_SLAB, -1)
    return jnp.concatenate([low_first, high_first, low_second, high_second], axis=-1)


def by_index(values, number):
    lead = values.shape[:-5]
    groups = number.shape[0]
    flat_number = number.reshape(groups * N_SLAB, -1)
    flat_values = values.reshape((-1, groups * N_SLAB, flat_number.shape[1]))

    def place(entries, targets):
        return jnp.zeros_like(entries).at[:, targets].set(entries)
    placed = jax.vmap(place, in_axes=(1, 0), out_axes=1)(flat_values, flat_number)
    return placed.reshape(lead + (groups, N_SLAB, -1))


def spread(values, level):
    lead_count = values.ndim - 3
    repeated = jnp.repeat(values, 1 << level, axis=lead_count)
    return repeated.reshape(values.shape[:lead_count] + (-1,))


def hierarchy(key):
    number_zero = level_numbering(key, 0)
    number_one = level_numbering(key, 1)
    number_two = level_numbering(key, 2)
    span_x, span_y, span_z, groups = level_shape(0)
    distance = jax.random.randint(jax.random.fold_in(key, 200), (7, groups, N_SLAB, span_x, span_y, span_z), 1, 3).astype(jnp.int32)
    unit = [1] * 7
    tables = {}
    tables['columns'] = spread(by_index(level_links(number_zero, 0, distance), number_zero), 0)
    tables['slots'] = spread(by_index(level_slots(0, distance), number_zero), 0)
    tables['aggregates'] = spread(by_index(level_aggregates(0, number_one), number_zero), 0)
    tables['sends'] = spread(level_sends(number_zero, 0), 0)
    tables['columns_one'] = spread(by_index(level_links(number_one, 1, unit), number_one), 1)
    tables['slots_one'] = spread(by_index(level_slots(1, unit), number_one), 1)
    tables['aggregates_one'] = spread(by_index(level_aggregates(1, number_two), number_one), 1)
    tables['sends_one'] = spread(level_sends(number_one, 1), 1)
    tables['columns_two'] = spread(by_index(level_links(number_two, 2, unit), number_two), 2)
    tables['sends_two'] = spread(level_sends(number_two, 2), 2)
    return tables


def draw_columns(key, part):
    return hierarchy(key)['columns']


def draw_slots(key, part):
    return hierarchy(key)['slots']


def draw_aggregates(key, part):
    return hierarchy(key)['aggregates']


def draw_sends(key, part):
    return hierarchy(key)['sends']


def draw_columns_one(key, part):
    return hierarchy(key)['columns_one']


def draw_slots_one(key, part):
    return hierarchy(key)['slots_one']


def draw_aggregates_one(key, part):
    return hierarchy(key)['aggregates_one']


def draw_sends_one(key, part):
    return hierarchy(key)['sends_one']


def draw_columns_two(key, part):
    return hierarchy(key)['columns_two']


def draw_sends_two(key, part):
    return hierarchy(key)['sends_two']


def draw_prolong_one(key, part):
    span_x, span_y, span_z, groups = level_shape(1)
    shape = (4, 4, groups, N_SLAB, span_x * span_y * span_z)
    subkey = jax.random.fold_in(key, 300)
    values = 0.35 * jnp.clip(jax.random.normal(subkey, shape, jnp.float32), -5.0, 5.0)
    return spread(values, 1)


def draw_operator(key, part):
    count = GX * GY * GZ * N_SUB * N_SLAB
    subkeys = jax.random.split(jax.random.fold_in(key, 400), 4)
    noise = jnp.clip(jax.random.normal(subkeys[0], (7, 4, 4, count), jnp.float32), -4.0, 4.0)
    scale = jnp.ones((1, 4, 1, count), jnp.float32)
    identity = jnp.eye(4, dtype=jnp.float32).reshape(1, 4, 4, 1)
    centre = jnp.exp(jax.random.uniform(subkeys[1], (1, 4, 1, count), jnp.float32, 1.79, 2.64))
    couple = jax.random.uniform(subkeys[2], (6, 4, 1, count), jnp.float32, 0.4, 1.6)
    first = centre * identity + 0.6 * noise[:1] * (1.0 - identity)
    rest = -couple * identity + 0.35 * noise[1:]
    return scale * jnp.concatenate([first, rest], axis=0)


def steps_of(key, shape, shards, least, largest):
    def one(axis_at, blocks):
        draws = jax.random.uniform(jax.random.fold_in(jax.random.fold_in(key, 6), axis_at), (blocks,), jnp.float32, least / len(shards), largest / len(shards))
        return jnp.repeat(jnp.exp(draws), shape[axis_at] // blocks).reshape((-1,) + (1,) * (len(shape) - axis_at - 1))

    gain = one(*shards[0])
    for cut in shards[1:]:
        gain = gain * one(*cut)
    return gain


def centred(rng, extent, width, reach, pieces=(), held_as=jnp.bfloat16):
    drawn = jax.random.normal(rng, extent, jnp.float32) * width
    if len(pieces) > 0:
        drawn = steps_of(rng, extent, pieces, -0.22, 0.18) * drawn
    return jnp.clip(drawn, min=-reach, max=reach).astype(held_as)


def setup_inputs(seed: int = 0) -> dict:
    seeds = jax.random.split(jax.random.key(seed), 15)
    return {
        "source": centred(seeds[0], (4, CELLS * DEVICES), 1.0, 6.0, ((1, 32),), jnp.float32),
        "operator": draw_operator(jax.random.fold_in(seeds[14], 71), 0),
        "prolong": centred(seeds[2], (4, 4, CELLS * DEVICES), 0.35, 2.0, ((2, 32),), jnp.float32),
        "columns": draw_columns(jax.random.fold_in(seeds[14], 71), 0),
        "slots": draw_slots(jax.random.fold_in(seeds[14], 71), 0),
        "aggregates": draw_aggregates(jax.random.fold_in(seeds[14], 71), 0),
        "sends": draw_sends(jax.random.fold_in(seeds[14], 71), 0),
        "prolong_one": draw_prolong_one(jax.random.fold_in(seeds[14], 71), 0),
        "columns_one": draw_columns_one(jax.random.fold_in(seeds[14], 71), 0),
        "slots_one": draw_slots_one(jax.random.fold_in(seeds[14], 71), 0),
        "aggregates_one": draw_aggregates_one(jax.random.fold_in(seeds[14], 71), 0),
        "sends_one": draw_sends_one(jax.random.fold_in(seeds[14], 71), 0),
        "columns_two": draw_columns_two(jax.random.fold_in(seeds[14], 71), 0),
        "sends_two": draw_sends_two(jax.random.fold_in(seeds[14], 71), 0),
    }


def apply_rows(operator, columns, extended):
    nearby = extended[:, columns]
    total = jnp.zeros_like(operator[0, :, 0, :])
    for comp in range(4):
        total = total + jnp.sum(operator[:, :, comp, :] * nearby[comp][:, None, :], axis=0)
    return total


def row_weights(operator):
    return 1.0 + jnp.sum(jnp.abs(operator), axis=(0, 2))


def restrict_rows(prolong, residual, aggregates, coarse):
    lifted = jnp.sum(prolong * residual[:, None, :], axis=0)
    return jnp.zeros((4, coarse), lifted.dtype).at[:, aggregates].add(lifted)


def galerkin_rows(operator, prolong, columns, slots, aggregates, extended, coarse):
    nearby = extended[:, :, columns]
    inner = jnp.zeros((4,) + nearby.shape[1:], nearby.dtype)
    for comp in range(4):
        inner = inner + jnp.transpose(operator[:, :, comp, :], (1, 0, 2))[:, None, :, :] * nearby[comp][None]
    blocks = jnp.zeros_like(inner)
    for comp in range(4):
        blocks = blocks + prolong[comp][:, None, None, :] * inner[comp][None]
    target = (slots * coarse + aggregates[None, :]).reshape(-1)
    total = jnp.zeros((16, 7 * coarse), blocks.dtype).at[:, target].add(blocks.reshape(16, -1))
    return total.reshape(4, 4, 7, coarse).transpose(2, 0, 1, 3)


def to_devices(array):
    lead = array.shape[:-1]
    shaped = array.reshape(lead + (N_SUB, N_SLAB, -1))
    return jnp.moveaxis(shaped, (len(lead), len(lead) + 1), (0, 1))


def from_devices(array):
    moved = jnp.moveaxis(array, (0, 1), (-3, -2))
    return moved.reshape(moved.shape[:-3] + (-1,))


def shift_devices(array, axis, offset):
    rolled = jnp.roll(array, offset, axis=axis)
    count = array.shape[axis]
    anchor = jnp.arange(count) - offset
    valid = (anchor >= 0) & (anchor < count)
    shape = [1] * array.ndim
    shape[axis] = count
    return jnp.where(valid.reshape(shape), rolled, jnp.zeros_like(rolled))


def per_device(function):
    return jax.vmap(jax.vmap(function))


def take_rows(values, sends):
    return values[:, sends]


def extend_all(values, sends, faces, group):
    first_count, second_count = faces
    picked = per_device(take_rows)(values, sends)
    low_first = picked[..., :first_count]
    high_first = picked[..., first_count:2 * first_count]
    low_second = picked[..., 2 * first_count:2 * first_count + second_count]
    high_second = picked[..., 2 * first_count + second_count:]
    parts = [values, shift_devices(high_first, 1, 1), shift_devices(low_first, 1, -1),
             shift_devices(high_second, 0, group), shift_devices(low_second, 0, -group)]
    return jnp.concatenate(parts, axis=-1)


def smooth_all(operator, columns, source, sends, faces, group, final):
    weights = per_device(row_weights)(operator)
    first = source / weights
    residual = source - per_device(apply_rows)(operator, columns, extend_all(first, sends, faces, group))
    second = first + residual / weights
    if final:
        residual = source - per_device(apply_rows)(operator, columns, extend_all(second, sends, faces, group))
    return second, residual


def flatten_lead(array):
    return array.reshape((-1,) + array.shape[2:])


def galerkin_all(operator, prolong, columns, slots, aggregates, sends, faces, group, coarse):
    lead = operator.shape[:2]
    flat_prolong = prolong.reshape(lead + (16, -1))
    extended = extend_all(flat_prolong, sends, faces, group)
    extended = extended.reshape(lead + (4, 4, -1))

    def single(items):
        return galerkin_rows(items[0], items[1], items[2], items[3], items[4], items[5], coarse)

    items = tuple(flatten_lead(item) for item in (operator, prolong, columns, slots, aggregates, extended))
    result = lax.map(single, items)
    return result.reshape(lead + result.shape[1:])


def merge_devices(array, bit):
    count = array.shape[0]
    stride = 1 << bit
    shaped = array.reshape((count // (2 * stride), 2, stride) + array.shape[1:])
    joined = jnp.concatenate([shaped[:, 0], shaped[:, 1]], axis=-1)
    spread = jnp.broadcast_to(joined[:, None], (joined.shape[0], 2) + joined.shape[1:])
    return spread.reshape((count,) + joined.shape[2:])


def own_share(array, members):
    count = array.shape[0]
    shaped = array.reshape((count // members, members) + array.shape[1:-1] + (members, -1))
    picked = [shaped[:, member, ..., member, :] for member in range(members)]
    stacked = jnp.stack(picked, axis=1)
    return stacked.reshape((count,) + stacked.shape[2:])


def reference(source, operator, prolong, columns, slots, aggregates, sends, prolong_one, columns_one, slots_one, aggregates_one, sends_one, columns_two, sends_two):
    faces_zero = (2 * GY * GZ, 2 * GX * GZ)
    faces_one = (GY * (GZ // 2), (GX // 2) * (GZ // 2))
    faces_two = (GY * (GZ // 4), (GX // 4) * (GZ // 4))
    rows_one = GX * GY * GZ // 8
    coarse_two = rows_one // 4
    source_dev = to_devices(source)
    operator_dev = to_devices(operator)
    prolong_dev = to_devices(prolong)
    columns_dev = to_devices(columns)
    slots_dev = to_devices(slots)
    aggregates_dev = to_devices(aggregates)
    sends_dev = to_devices(sends)
    prolong_one_dev = to_devices(prolong_one)
    columns_one_dev = to_devices(columns_one)
    slots_one_dev = to_devices(slots_one)
    aggregates_one_dev = to_devices(aggregates_one)
    sends_one_dev = to_devices(sends_one)
    columns_two_dev = to_devices(columns_two)
    sends_two_dev = to_devices(sends_two)

    smoothed, residual = smooth_all(operator_dev, columns_dev, source_dev, sends_dev, faces_zero, 1, True)
    source_own = per_device(partial(restrict_rows, coarse=rows_one))(prolong_dev, residual, aggregates_dev)
    operator_own = galerkin_all(operator_dev, prolong_dev, columns_dev, slots_dev, aggregates_dev, sends_dev, faces_zero, 1, rows_one)
    source_merged = merge_devices(source_own, 0)
    operator_merged = merge_devices(operator_own, 0)
    smooth_one, residual_one = smooth_all(operator_merged, columns_one_dev, source_merged, sends_one_dev, faces_one, 2, True)
    source_pair = per_device(partial(restrict_rows, coarse=coarse_two))(prolong_one_dev, residual_one, aggregates_one_dev)
    operator_pair = galerkin_all(operator_merged, prolong_one_dev, columns_one_dev, slots_one_dev, aggregates_one_dev, sends_one_dev, faces_one, 2, coarse_two)
    source_group = merge_devices(source_pair, 1)
    operator_group = merge_devices(operator_pair, 1)
    smooth_two, unused = smooth_all(operator_group, columns_two_dev, source_group, sends_two_dev, faces_two, 4, False)
    return from_devices(smoothed), from_devices(own_share(smooth_one, 2)), from_devices(own_share(smooth_two, 4))
```

```python
import functools

import jax
import jax.numpy as jnp
from jax import lax
from jax.experimental import pallas as pl
from jax.experimental.pallas import tpu as pltpu
from jax.sharding import PartitionSpec as P

GX = 8
GY = 8
GZ = 32
LANES = 128
F32 = jnp.float32
BF16 = jnp.bfloat16


def split(value):
    high = value.astype(BF16)
    return high, (value - high.astype(F32)).astype(BF16)


def upper_half(shape):
    return lax.broadcasted_iota(jnp.int32, shape, 0) >= 4


def fold(value):
    return value + pltpu.roll(value, 4, 0)


def pair_rows(first, second):
    return jnp.where(upper_half(first.shape), second, first)


def twice(rows):
    return jnp.concatenate([rows, rows], axis=0)


def table_four(chunks):
    if len(chunks) % 2:
        chunks = chunks + [jnp.zeros_like(chunks[0])]
    rows = [pair_rows(chunks[j], chunks[j + 1]) for j in range(0, len(chunks), 2)]
    return jnp.concatenate(split(jnp.concatenate(rows, axis=0)), axis=1)


def table_sixteen(chunks):
    return jnp.concatenate(split(jnp.concatenate(chunks, axis=0)), axis=1)


def onehot(columns):
    low = jnp.broadcast_to(columns & (LANES - 1), (LANES, columns.shape[1]))
    hot = (lax.broadcasted_iota(jnp.int32, low.shape, 0) == low).astype(F32).astype(BF16)
    return twice(hot)


def choose_four(picked, high):
    shape = (8, picked.shape[1])
    high = jnp.broadcast_to(high, shape) - upper_half(shape).astype(jnp.int32)
    total = jnp.zeros(shape, F32)
    for j in range(picked.shape[0] // 8):
        total = jnp.where(high == 2 * j, picked[8 * j : 8 * j + 8], total)
    return fold(total)


def choose_sixteen(picked, high):
    shape = (8, picked.shape[1])
    high = jnp.broadcast_to(high, shape)
    total = [jnp.zeros(shape, F32), jnp.zeros(shape, F32)]
    for j in range(picked.shape[0] // 16):
        here = high == j
        for half in range(2):
            at = 16 * j + 8 * half
            total[half] = jnp.where(here, picked[at : at + 8], total[half])
    return total


def matmul(left, right):
    return jnp.dot(left, right, preferred_element_type=F32)


def gather_four(table, columns):
    return choose_four(matmul(table, onehot(columns)), columns >> 7)


def gather_sixteen(table, columns):
    return jnp.concatenate(choose_sixteen(matmul(table, onehot(columns)), columns >> 7), axis=0)


def sum_components(value):
    first = value.astype(BF16)
    rest = value - first.astype(F32)
    second = rest.astype(BF16)
    third = (rest - second.astype(F32)).astype(BF16)
    row = lax.broadcasted_iota(jnp.int32, (8, 48), 0) & 3
    column = (lax.broadcasted_iota(jnp.int32, (8, 48), 1) >> 2) & 3
    ones = (row == column).astype(F32).astype(BF16)
    return matmul(ones, jnp.concatenate([first, second, third], axis=0))


def row_weights(operator_at):
    total = jnp.abs(operator_at(0))
    for k in range(1, 7):
        total = total + jnp.abs(operator_at(k))
    return 1.0 + sum_components(total)


def spread_row(value, row, rows=8):
    return jnp.broadcast_to(value[row : row + 1], (rows, value.shape[1]))


def lift(prolong, residual):
    low = pair_rows(spread_row(residual, 0), spread_row(residual, 1))
    high = pair_rows(spread_row(residual, 2), spread_row(residual, 3))
    return fold(prolong[:8] * low + prolong[8:] * high)


def expand(rows):
    return [
        [pair_rows(spread_row(rows, 4 * a + 2 * h), spread_row(rows, 4 * a + 2 * h + 1)) for h in (0, 1)]
        for a in range(4)
    ]


def triple_product(wide_prolong, operator, near):
    wide = expand(operator)
    out = [None, None]
    for a in range(4):
        inner = fold(wide[a][0] * near[0] + wide[a][1] * near[1])
        for half in range(2):
            term = wide_prolong[a][half] * inner
            out[half] = term if out[half] is None else out[half] + term
    return out


def scatter(values, targets, count):
    high, low = split(values)
    shape = (count, values.shape[1])
    hot = lax.broadcasted_iota(jnp.int32, shape, 0) == jnp.broadcast_to(targets, shape)
    hot = hot.astype(F32).astype(BF16)
    both = lax.dot_general(
        jnp.concatenate([high, low], axis=0),
        hot,
        (((1,), (1,)), ((), ())),
        preferred_element_type=F32,
    )
    rows = values.shape[0]
    return both[:rows] + both[rows:]


def chunks_of(value):
    return [value[:, at : at + LANES] for at in range(0, value.shape[1], LANES)]


def place():
    sub, slab = lax.axis_index("sub"), lax.axis_index("slab")
    return sub, slab


def neighbours(index, count, even, odd):
    is_even = index % 2 == 0
    if odd is None:
        odd = jnp.zeros_like(even)
    below = jnp.where(is_even, odd, even)
    above = jnp.where(is_even, even, odd)
    below = jnp.where(index > 0, below, jnp.zeros_like(below))
    above = jnp.where(index < count - 1, above, jnp.zeros_like(above))
    return below, above


def swap_halves(below, above, half):
    lane = lax.broadcasted_iota(jnp.int32, below.shape, 1)
    return pltpu.roll(jnp.where(lane < half, above, below), half, 1)


def call(body, outs, *args, scratch=()):
    return pl.pallas_call(
        body,
        out_shape=[jax.ShapeDtypeStruct(shape, F32) for shape in outs],
        in_specs=[pl.BlockSpec(memory_space=pltpu.VMEM)] * len(args),
        out_specs=[pl.BlockSpec(memory_space=pltpu.VMEM)] * len(outs),
        scratch_shapes=list(scratch),
        compiler_params=pltpu.CompilerParams(vmem_limit_bytes=48 * 1024 * 1024),
    )(*args)


TILE = 256


def tiles(count, body):
    def step(index, carry):
        body(pl.ds(pl.multiple_of(index * TILE, TILE), TILE))
        return carry

    lax.fori_loop(0, count // TILE, step, 0)


def fine_first(
    source, operator, prolong, sends, prolong_one, sends_one, w_ref, first_ref, *rest
):
    picks = rest[-1]
    parity_out, cross_out, slab_outs = rest[0], rest[1], rest[2:-1]
    weights = row_weights(lambda k: operator[16 * k : 16 * k + 16])
    first = twice(source[...]) / weights
    w_ref[...] = weights
    first_ref[...] = first
    table = jnp.concatenate(
        [table_four(chunks_of(first)), table_sixteen(chunks_of(prolong[...]))], axis=0
    )
    split_at = first.shape[1] // LANES * 4

    def pick(at):
        columns = sends[:, at]
        picked = matmul(table, onehot(columns))
        picks[0:8, at] = choose_four(picked[:split_at], columns >> 7)
        low, high = choose_sixteen(picked[split_at:], columns >> 7)
        picks[8:16, at] = low
        picks[16:24, at] = high

    tiles(sends.shape[1], pick)
    coarse = gather_sixteen(table_sixteen(chunks_of(prolong_one[...])), sends_one[...])
    sub, slab = place()
    count = sends.shape[1] // 4
    low_first, high_first = picks[:, 0:count], picks[:, count : 2 * count]
    low_second, high_second = picks[:, 2 * count : 3 * count], picks[:, 3 * count :]
    even = sub % 2 == 0
    parity_out[...] = jnp.where(even, high_second, low_second)
    cross_out[:, 0:count] = jnp.where(even, low_second, high_second)
    cross_out[0:16, count:] = coarse[:, 2 * LANES :]
    cross_out[16:24, count:] = jnp.zeros((8, LANES), F32)
    slab_even = slab % 2 == 0
    for position, out in enumerate(slab_outs):
        up = slab_even if position == 0 else jnp.logical_not(slab_even)
        out[:, 0:count] = jnp.where(up, high_first, low_first)
        out[0:16, count:] = jnp.where(up, coarse[:, LANES : 2 * LANES], coarse[:, 0:LANES])
        out[16:24, count:] = jnp.zeros((8, LANES), F32)


def fine_ghosts(rows, count, sizes, parity_in, cross_in, slab_ins):
    sub, slab = place()
    at = slice(0, count)
    slab_values = [ref[rows, at] for ref in slab_ins] + [None]
    below, above = neighbours(slab, sizes[1], slab_values[0], slab_values[1])
    left, right = neighbours(sub, sizes[0], parity_in[rows, at], cross_in[rows, at])
    return chunks_of(below) + chunks_of(above) + chunks_of(left) + chunks_of(right)


def apply_tile(table, operator, columns, at):
    total = None
    for k in range(7):
        near = twice(gather_four(table, columns[k : k + 1, at]))
        term = operator[16 * k : 16 * k + 16, at] * near
        total = term if total is None else total + term
    return sum_components(total)


def fine_second(
    sizes, source, operator, columns, sends, w_ref, first_ref, parity_in, cross_in, *rest
):
    slab_count = (len(rest) - 5) // 2
    slab_ins, rest = rest[:slab_count], rest[slab_count:]
    smoothed, parity_out, cross_out = rest[0], rest[1], rest[2]
    slab_outs, second_ref, picks = rest[3:-2], rest[-2], rest[-1]
    count = sends.shape[1] // 4
    ghosts = fine_ghosts(slice(0, 8), count, sizes, parity_in, cross_in, slab_ins)
    table = table_four(chunks_of(first_ref[...]) + ghosts)

    def step(at):
        residual = twice(source[:, at]) - apply_tile(table, operator, columns, at)
        second_ref[:, at] = first_ref[:, at] + residual / w_ref[:, at]

    tiles(source.shape[1], step)
    smoothed[...] = second_ref[0:4]
    table = table_four(chunks_of(second_ref[...]))

    def pick(at):
        picks[:, at] = gather_four(table, sends[:, at])

    tiles(sends.shape[1], pick)
    sub, slab = place()
    low_first, high_first = picks[:, 0:count], picks[:, count : 2 * count]
    low_second, high_second = picks[:, 2 * count : 3 * count], picks[:, 3 * count :]
    even = sub % 2 == 0
    parity_out[:, 0:count] = jnp.where(even, high_second, low_second)
    parity_out[:, count : count + LANES] = cross_in[0:8, count:]
    parity_out[:, count + LANES :] = cross_in[8:16, count:]
    cross_out[...] = jnp.where(even, low_second, high_second)
    slab_even = slab % 2 == 0
    for position, out in enumerate(slab_outs):
        up = slab_even if position == 0 else jnp.logical_not(slab_even)
        out[...] = jnp.where(up, high_first, low_first)


def coarsen(table, operator, prolong, columns, slots, aggregates, sums, count):
    def step(at):
        wide_prolong = expand(prolong[:, at])
        totals = [[jnp.zeros((8, TILE), F32) for _ in range(2)] for _ in range(7)]
        for k in range(7):
            column = columns[k : k + 1, at]
            near = choose_sixteen(matmul(table, onehot(column)), column >> 7)
            blocks = triple_product(wide_prolong, operator[16 * k : 16 * k + 16, at], near)
            slot = jnp.broadcast_to(slots[k : k + 1, at], (8, TILE))
            for s in range(7):
                here = slot == s
                for half in range(2):
                    totals[s][half] = totals[s][half] + jnp.where(here, blocks[half], 0.0)
        for s in range(7):
            for half in range(2):
                row = 16 * s + 8 * half
                sums[row : row + 8, at] = totals[s][half]

    tiles(columns.shape[1], step)
    return scatter(sums[...], aggregates[...], count)


def fine_coarsen(
    sizes,
    source,
    operator,
    prolong,
    columns,
    slots,
    aggregates,
    second_ref,
    parity_old,
    cross_old,
    parity_in,
    cross_in,
    *rest,
):
    slab_count = (len(rest) - 3) // 2
    slab_old, slab_ins, rest = rest[:slab_count], rest[slab_count : 2 * slab_count], rest[-3:]
    out, sums, lifted = rest
    count = parity_old.shape[1]
    ghosts = fine_ghosts(slice(0, 8), count, sizes, parity_in, cross_in, slab_ins)
    table = table_four(chunks_of(second_ref[...]) + ghosts)

    def step(at):
        residual = twice(source[:, at]) - apply_tile(table, operator, columns, at)
        lifted[:, at] = lift(prolong[:, at], residual)

    tiles(source.shape[1], step)
    rows = out.shape[1]
    out[112:120] = scatter(lifted[...], aggregates[...], rows)
    ghosts = fine_ghosts(slice(8, 24), count, sizes, parity_old, cross_old, slab_old)
    table = table_sixteen(chunks_of(prolong[...]) + ghosts)
    out[0:112] = coarsen(table, operator, prolong, columns, slots, aggregates, sums, rows)


def slab_faces(picks, slab, slab_outs):
    slab_even = slab % 2 == 0
    for position, out in enumerate(slab_outs):
        up = slab_even if position == 0 else jnp.logical_not(slab_even)
        out[...] = jnp.where(up, picks[:, LANES : 2 * LANES], picks[:, 0:LANES])


def pair_first(own, other, sends, operator, source, weights, first, group_out, *slab_outs):
    sub, slab = place()
    even = sub % 2 == 0
    half = own.shape[1]
    lower = jnp.where(even, own[...], other[...])
    upper = jnp.where(even, other[...], own[...])
    operator[:, 0:half] = lower[0:112]
    operator[:, half:] = upper[0:112]
    source[:, 0:half] = lower[112:120]
    source[:, half:] = upper[112:120]
    weights[...] = row_weights(lambda k: operator[16 * k : 16 * k + 16])
    first[...] = source[...] / weights[...]
    picks = gather_four(table_four(chunks_of(first[...])), sends[...])
    group_out[...] = picks[:, 2 * LANES :]
    slab_faces(picks, slab, slab_outs)


def pair_ghosts(sizes, even_in, odd_in, slab_ins):
    sub, slab = place()
    values = [ref[...] for ref in slab_ins] + [None]
    below, above = neighbours(slab, sizes[1], values[0], values[1])
    left, right = neighbours(sub // 2, sizes[0] // 2, even_in[...], odd_in[...])
    return [below, above, swap_halves(left, right, LANES // 2)]


def pair_second(
    sizes, operator, source, weights, first, columns, sends, even_in, odd_in, *rest
):
    slab_count = (len(rest) - 3) // 2
    slab_ins, rest = rest[:slab_count], rest[slab_count:]
    smoothed, second_ref, group_out = rest[0], rest[1], rest[2]
    slab_outs = rest[3:]
    table = table_four(chunks_of(first[...]) + pair_ghosts(sizes, even_in, odd_in, slab_ins))

    def step(at):
        residual = source[:, at] - apply_tile(table, operator, columns, at)
        second_ref[:, at] = first[:, at] + residual / weights[:, at]

    tiles(source.shape[1], step)
    sub, slab = place()
    half = smoothed.shape[1]
    smoothed[...] = jnp.where(sub % 2 == 0, second_ref[0:4, 0:half], second_ref[0:4, half:])
    picks = gather_four(table_four(chunks_of(second_ref[...])), sends[...])
    group_out[...] = picks[:, 2 * LANES :]
    slab_faces(picks, slab, slab_outs)


def pair_coarsen(
    sizes,
    operator,
    source,
    second_ref,
    prolong,
    columns,
    slots,
    aggregates,
    sends,
    parity_old,
    cross_old,
    forwarded,
    even_in,
    odd_in,
    *rest,
):
    slab_count = (len(rest) - 6) // 2
    slab_old, slab_ins, rest = rest[:slab_count], rest[slab_count : 2 * slab_count], rest[-6:]
    message, operator_two, source_two, first_two, sums, lifted = rest
    sub, slab = place()
    even = sub % 2 == 0
    table = table_four(chunks_of(second_ref[...]) + pair_ghosts(sizes, even_in, odd_in, slab_ins))

    def step(at):
        residual = source[:, at] - apply_tile(table, operator, columns, at)
        lifted[:, at] = lift(prolong[:, at], residual)

    tiles(source.shape[1], step)
    source_two[...] = scatter(lifted[...], aggregates[...], LANES)

    count = parity_old.shape[1]
    values = [ref[0:16, count:] for ref in slab_old] + [None]
    below, above = neighbours(slab, sizes[1], values[0], values[1])
    mine = cross_old[0:16, count:]
    partners = jnp.concatenate(
        [forwarded[:, count : count + LANES], forwarded[:, count + LANES :]], axis=0
    )
    group = sub // 2
    left = jnp.where(even, mine, partners)
    right = jnp.where(even, partners, mine)
    left = jnp.where(group > 0, left, jnp.zeros_like(left))
    right = jnp.where(group < sizes[0] // 2 - 1, right, jnp.zeros_like(right))
    ghosts = [below, above, swap_halves(left, right, LANES // 2)]
    table = table_sixteen(chunks_of(prolong[...]) + ghosts)
    operator_two[...] = coarsen(
        table, operator, prolong, columns, slots, aggregates, sums, LANES
    )
    first = source_two[...] / row_weights(lambda k: operator_two[16 * k : 16 * k + 16])
    first_two[...] = first
    lane = lax.broadcasted_iota(jnp.int32, first.shape, 1)
    first = jnp.where(lane < LANES // 2, first, 0.0)
    placed = jnp.where(group % 2 == 0, first, pltpu.roll(first, LANES // 2, 1))
    picks = gather_four(table_four([placed]), sends[...])
    faces = picks[:, 0:LANES]
    seconds = pltpu.roll(picks[:, LANES:], LANES // 2, 1)
    sent = pair_rows(jnp.where(lane < LANES // 2, first, seconds), faces)
    message[...] = jnp.broadcast_to(sent[None], message.shape)


def group_second(sizes, operator, source, first_two, columns, received, out):
    sub, slab = place()
    subs, slabs = sizes
    group, pair = sub // 4, sub // 2 % 2
    shape = (8, LANES)
    lane = lax.broadcasted_iota(jnp.int32, shape, 1)
    half = LANES // 2

    def from_pair(group_at, pair_at, slab_at):
        valid = (group_at >= 0) & (group_at < subs // 4) & (slab_at >= 0) & (slab_at < slabs)
        index = (group_at * 4 + pair_at * 2 + sub % 2) * slabs + slab_at
        index = jnp.where(valid, index, 0)
        return jnp.where(valid, received[index], jnp.zeros(shape, F32))

    def from_group(group_at, slab_at):
        return from_pair(group_at, 0, slab_at) + from_pair(group_at, 1, slab_at)

    def lower(value):
        return pair_rows(value, pltpu.roll(value, 4, 0))

    def upper(value):
        return pair_rows(pltpu.roll(value, 4, 0), value)

    pairs = [lower(from_pair(group, j, slab)) for j in range(2)]
    first = jnp.where(lane < half, pairs[0], pltpu.roll(pairs[1], half, 1))
    firsts = swap_halves(
        upper(from_group(group, slab - 1)), upper(from_group(group, slab + 1)), half
    )
    width = GX // 4 * (GZ // 4)
    left = lower(from_group(group - 1, slab))
    right = lower(from_group(group + 1, slab))
    seconds = jnp.where(
        lane < width,
        pltpu.roll(left, LANES - half - width, 1),
        pltpu.roll(right, LANES - half + width, 1),
    )
    seconds = jnp.where(lane < 2 * width, seconds, 0.0)
    table = table_four([first, firsts, seconds])
    mine = jnp.where(pair == 0, columns[...], pltpu.roll(columns[...], half, 1))
    total = None
    for k in range(7):
        near = twice(gather_four(table, mine[k : k + 1]))
        term = operator[16 * k : 16 * k + 16] * near
        total = term if total is None else total + term
    residual = source[...] - sum_components(total)
    weights = row_weights(lambda k: operator[16 * k : 16 * k + 16])
    second = first_two[...] + residual / weights
    share = out.shape[1]
    out[...] = jnp.where(sub % 2 == 0, second[0:4, 0:share], second[0:4, share : 2 * share])


def pairing(value, axis, group, odd):
    count = lax.axis_size(axis)
    blocks = count // group
    route = []
    for index in range(count):
        block = index // group
        mate = ((block - 1) ^ 1) + 1 if odd else block ^ 1
        route.append((index, mate % blocks * group + index % group))
    return lax.ppermute(value, axis, route)


def slab_pairings(values):
    return [pairing(value, "slab", 1, position == 1) for position, value in enumerate(values)]


def on_device(
    source,
    operator,
    prolong,
    columns,
    slots,
    aggregates,
    sends,
    prolong_one,
    columns_one,
    slots_one,
    aggregates_one,
    sends_one,
    columns_two,
    sends_two,
):
    sizes = (lax.axis_size("sub"), lax.axis_size("slab"))
    slab_moves = 1 if sizes[1] == 2 else 2
    rows = source.shape[1]
    rows_one = rows // 8
    pair_rows_one = 2 * rows_one
    count = 2 * GY * GZ
    operator = operator.reshape(112, rows)
    prolong = prolong.reshape(16, rows)
    prolong_one = prolong_one.reshape(16, pair_rows_one)
    sends = sends.reshape(1, -1)
    sends_one = sends_one.reshape(1, -1)
    aggregates = aggregates.reshape(1, -1)
    aggregates_one = aggregates_one.reshape(1, -1)
    sends_two = jnp.pad(sends_two, (0, -sends_two.shape[0] % LANES)).reshape(1, -1)

    weights, first, even, odd, *slabs = call(
        fine_first,
        [(8, rows), (8, rows), (24, count), (24, count + LANES)]
        + [(24, count + LANES)] * slab_moves,
        source,
        operator,
        prolong,
        sends,
        prolong_one,
        sends_one,
        scratch=[pltpu.VMEM((24, sends.shape[1]), F32)],
    )
    even_old = pairing(even, "sub", 1, False)
    odd_old = pairing(odd, "sub", 1, True)
    slabs_old = slab_pairings(slabs)

    smoothed, even, odd, *rest = call(
        functools.partial(fine_second, sizes),
        [(4, rows), (8, count + 2 * LANES), (8, count)]
        + [(8, count)] * slab_moves
        + [(8, rows)],
        source,
        operator,
        columns,
        sends,
        weights,
        first,
        even_old,
        odd_old,
        *slabs_old,
        scratch=[pltpu.VMEM((8, sends.shape[1]), F32)],
    )
    slabs, second = rest[:-1], rest[-1]
    forwarded = pairing(even, "sub", 1, False)
    odd_in = pairing(odd, "sub", 1, True)
    slabs_in = slab_pairings(slabs)

    (own,) = call(
        functools.partial(fine_coarsen, sizes),
        [(120, rows_one)],
        source,
        operator,
        prolong,
        columns,
        slots,
        aggregates,
        second,
        even_old,
        odd_old,
        forwarded,
        odd_in,
        *slabs_old,
        *slabs_in,
        scratch=[pltpu.VMEM((112, rows), F32), pltpu.VMEM((8, rows), F32)],
    )
    other = pairing(own, "sub", 1, False)

    faces = [(8, LANES)] * (1 + slab_moves)
    operator_one, source_one, weights_one, first_one, group_out, *slabs = call(
        pair_first,
        [(112, pair_rows_one)] + [(8, pair_rows_one)] * 3 + faces,
        own,
        other,
        sends_one,
    )
    even_in = pairing(group_out, "sub", 2, False)
    odd_in = pairing(group_out, "sub", 2, True)
    slabs_in = slab_pairings(slabs)

    smoothed_one, second_one, group_out, *slabs = call(
        functools.partial(pair_second, sizes),
        [(4, rows_one), (8, pair_rows_one)] + faces,
        operator_one,
        source_one,
        weights_one,
        first_one,
        columns_one,
        sends_one,
        even_in,
        odd_in,
        *slabs_in,
    )
    even_in = pairing(group_out, "sub", 2, False)
    odd_in = pairing(group_out, "sub", 2, True)
    slabs_in = slab_pairings(slabs)

    message, operator_two, source_two, first_two = call(
        functools.partial(pair_coarsen, sizes),
        [(sizes[0] * sizes[1], 8, LANES), (112, LANES), (8, LANES), (8, LANES)],
        operator_one,
        source_one,
        second_one,
        prolong_one,
        columns_one,
        slots_one,
        aggregates_one,
        sends_two,
        even_old,
        odd_old,
        forwarded,
        even_in,
        odd_in,
        *slabs_old,
        *slabs_in,
        scratch=[pltpu.VMEM((112, pair_rows_one), F32), pltpu.VMEM((8, pair_rows_one), F32)],
    )
    received = lax.all_to_all(message, ("sub", "slab"), 0, 0)

    (smoothed_two,) = call(
        functools.partial(group_second, sizes),
        [(4, rows_one // 8)],
        operator_two,
        source_two,
        first_two,
        columns_two,
        received,
    )
    return (smoothed, smoothed_one, smoothed_two)


def solution(mesh):
    placed = (
        P(None, ("sub", "slab")),
        P(None, None, None, ("sub", "slab")),
        P(None, None, ("sub", "slab")),
        P(None, ("sub", "slab")),
        P(None, ("sub", "slab")),
        P(("sub", "slab")),
        P(("sub", "slab")),
        P(None, None, ("sub", "slab")),
        P(None, ("sub", "slab")),
        P(None, ("sub", "slab")),
        P(("sub", "slab")),
        P(("sub", "slab")),
        P(None, ("sub", "slab")),
        P(("sub", "slab")),
    )
    return jax.shard_map(
        on_device,
        mesh=mesh,
        in_specs=placed,
        out_specs=(P(None, ("sub", "slab")), P(None, ("sub", "slab")), P(None, ("sub", "slab"))),
        check_vma=False,
    )
```

```python
import functools

import jax
import jax.numpy as jnp
from jax import lax
from jax.experimental import pallas as pl
from jax.experimental.pallas import tpu as pltpu
from jax.sharding import PartitionSpec as P

GX = 8
GY = 8
GZ = 32
LANES = 128
F32 = jnp.float32
BF16 = jnp.bfloat16


def split(value):
    high = value.astype(BF16)
    return high, (value - high.astype(F32)).astype(BF16)


def upper_half(shape):
    return lax.broadcasted_iota(jnp.int32, shape, 0) >= 4


def fold(value):
    return value + pltpu.roll(value, 4, 0)


def pair_rows(first, second):
    return jnp.where(upper_half(first.shape), second, first)


def twice(rows):
    return jnp.concatenate([rows, rows], axis=0)


def table_four(chunks):
    if len(chunks) % 2:
        chunks = chunks + [jnp.zeros_like(chunks[0])]
    rows = [pair_rows(chunks[j], chunks[j + 1]) for j in range(0, len(chunks), 2)]
    return jnp.concatenate(split(jnp.concatenate(rows, axis=0)), axis=1)


def table_sixteen(chunks):
    return jnp.concatenate(split(jnp.concatenate(chunks, axis=0)), axis=1)


def onehot(columns):
    low = (columns & (LANES - 1)).astype(jnp.int16)
    low = jnp.broadcast_to(low, (LANES, columns.shape[1]))
    here = lax.broadcasted_iota(jnp.int16, low.shape, 0) == low
    return twice(jnp.where(here, jnp.ones((), BF16), jnp.zeros((), BF16)))


def choose_four(picked, high):
    shape = (8, picked.shape[1])
    high = jnp.broadcast_to(high, shape) - upper_half(shape).astype(jnp.int32)
    total = jnp.zeros(shape, F32)
    for j in range(picked.shape[0] // 8):
        total = jnp.where(high == 2 * j, picked[8 * j : 8 * j + 8], total)
    return fold(total)


def choose_sixteen(picked, high):
    shape = (8, picked.shape[1])
    high = jnp.broadcast_to(high, shape)
    total = [jnp.zeros(shape, F32), jnp.zeros(shape, F32)]
    for j in range(picked.shape[0] // 16):
        here = high == j
        for half in range(2):
            at = 16 * j + 8 * half
            total[half] = jnp.where(here, picked[at : at + 8], total[half])
    return total


def matmul(left, right):
    return jnp.dot(left, right, preferred_element_type=F32)


def gather_four(table, columns):
    return choose_four(matmul(table, onehot(columns)), columns >> 7)


def gather_sixteen(table, columns):
    return jnp.concatenate(choose_sixteen(matmul(table, onehot(columns)), columns >> 7), axis=0)


def sum_components(value):
    first = value.astype(BF16)
    rest = value - first.astype(F32)
    second = rest.astype(BF16)
    third = (rest - second.astype(F32)).astype(BF16)
    row = lax.broadcasted_iota(jnp.int32, (8, 48), 0) & 3
    column = (lax.broadcasted_iota(jnp.int32, (8, 48), 1) >> 2) & 3
    ones = (row == column).astype(F32).astype(BF16)
    return matmul(ones, jnp.concatenate([first, second, third], axis=0))


def row_weights(operator_at):
    total = jnp.abs(operator_at(0))
    for k in range(1, 7):
        total = total + jnp.abs(operator_at(k))
    return 1.0 + sum_components(total)


def spread_row(value, row, rows=8):
    return jnp.broadcast_to(value[row : row + 1], (rows, value.shape[1]))


def lift(prolong, residual):
    low = pair_rows(spread_row(residual, 0), spread_row(residual, 1))
    high = pair_rows(spread_row(residual, 2), spread_row(residual, 3))
    return fold(prolong[:8] * low + prolong[8:] * high)


def expand(rows):
    return [
        [pair_rows(spread_row(rows, 4 * a + 2 * h), spread_row(rows, 4 * a + 2 * h + 1)) for h in (0, 1)]
        for a in range(4)
    ]


def triple_product(wide_prolong, operator, near):
    wide = expand(operator)
    out = [None, None]
    for a in range(4):
        inner = fold(wide[a][0] * near[0] + wide[a][1] * near[1])
        for half in range(2):
            term = wide_prolong[a][half] * inner
            out[half] = term if out[half] is None else out[half] + term
    return out


def scatter(values, targets, count):
    high, low = split(values)
    shape = (count, values.shape[1])
    hot = lax.broadcasted_iota(jnp.int32, shape, 0) == jnp.broadcast_to(targets, shape)
    hot = hot.astype(F32).astype(BF16)
    both = lax.dot_general(
        jnp.concatenate([high, low], axis=0),
        hot,
        (((1,), (1,)), ((), ())),
        preferred_element_type=F32,
    )
    rows = values.shape[0]
    return both[:rows] + both[rows:]


def chunks_of(value):
    return [value[:, at : at + LANES] for at in range(0, value.shape[1], LANES)]


def place():
    sub, slab = lax.axis_index("sub"), lax.axis_index("slab")
    return sub, slab


def neighbours(index, count, even, odd):
    is_even = index % 2 == 0
    if odd is None:
        odd = jnp.zeros_like(even)
    below = jnp.where(is_even, odd, even)
    above = jnp.where(is_even, even, odd)
    below = jnp.where(index > 0, below, jnp.zeros_like(below))
    above = jnp.where(index < count - 1, above, jnp.zeros_like(above))
    return below, above


def swap_halves(below, above, half):
    lane = lax.broadcasted_iota(jnp.int32, below.shape, 1)
    return pltpu.roll(jnp.where(lane < half, above, below), half, 1)


def call(body, outs, *args, scratch=(), flops=0, space=pltpu.VMEM):
    outs = [(out, F32) if isinstance(out[0], int) else out for out in outs]
    cost = pl.CostEstimate(flops=flops, bytes_accessed=0, transcendentals=0) if flops else None
    return pl.pallas_call(
        body,
        out_shape=[jax.ShapeDtypeStruct(shape, dtype) for shape, dtype in outs],
        in_specs=[pl.BlockSpec(memory_space=space)] * len(args),
        out_specs=[pl.BlockSpec(memory_space=pltpu.VMEM)] * len(outs),
        scratch_shapes=list(scratch),
        cost_estimate=cost,
        compiler_params=pltpu.CompilerParams(vmem_limit_bytes=32 * 1024 * 1024),
    )(*args)


def tiles(count, tile, body):
    def step(index, carry):
        body(pl.ds(pl.multiple_of(index * tile, tile), tile))
        return carry

    lax.fori_loop(0, count // tile, step, 0, unroll=True)


def fine_first(handed, slab_moves, *refs):
    count = handed + 3
    raw, refs = refs[:count], refs[count:]
    kept, refs = refs[:handed], refs[handed:]
    operator, prolong, prolong_one, w_ref, first_ref, parity_out, cross_out = refs[:7]
    slab_outs, refs = refs[7 : 7 + slab_moves], refs[7 + slab_moves :]
    operator_raw, prolong_raw, prolong_one_raw, picks, semaphores = refs
    source, sends, sends_one = kept[0], kept[1], kept[2]
    targets = [operator_raw, source, prolong_raw, sends, prolong_one_raw, sends_one, *kept[3:]]
    copies = [
        pltpu.make_async_copy(
            raw[at], target if raw[at].ndim > 1 else target.at[0], semaphores.at[at]
        )
        for at, target in enumerate(targets)
    ]
    for copy in copies:
        copy.start()
    copies[0].wait()
    sums = [None] * 4
    for k in range(7):
        for a in range(4):
            value = jnp.abs(operator_raw[k, a])
            sums[a] = value if sums[a] is None else sums[a] + value
    weights = 1.0 + sum_components(jnp.concatenate(sums, axis=0))
    copies[1].wait()
    first = twice(source[...]) / weights
    w_ref[...] = weights
    first_ref[...] = first
    for at in range(2, 6):
        copies[at].wait()
    for half in range(2):
        at = slice(8 * half, 8 * half + 8)
        prolong[at] = jnp.concatenate([prolong_raw[2 * half], prolong_raw[2 * half + 1]], axis=0)
        prolong_one[at] = jnp.concatenate(
            [prolong_one_raw[2 * half], prolong_one_raw[2 * half + 1]], axis=0
        )
    table = jnp.concatenate(
        [table_four(chunks_of(first)), table_sixteen(chunks_of(prolong[...]))], axis=0
    )
    split_at = first.shape[1] // LANES * 4

    def pick(at):
        columns = sends[:, at]
        picked = matmul(table, onehot(columns))
        picks[0:8, at] = choose_four(picked[:split_at], columns >> 7)
        low, high = choose_sixteen(picked[split_at:], columns >> 7)
        picks[8:16, at] = low
        picks[16:24, at] = high

    tiles(sends.shape[1], 512, pick)
    coarse = gather_sixteen(table_sixteen(chunks_of(prolong_one[...])), sends_one[...])
    sub, slab = place()
    count = sends.shape[1] // 4
    low_first, high_first = picks[:, 0:count], picks[:, count : 2 * count]
    low_second, high_second = picks[:, 2 * count : 3 * count], picks[:, 3 * count :]
    even = sub % 2 == 0
    parity_out[...] = jnp.where(even, high_second, low_second)
    cross_out[:, 0:count] = jnp.where(even, low_second, high_second)
    cross_out[0:16, count:] = coarse[:, 2 * LANES :]
    cross_out[16:24, count:] = jnp.zeros((8, LANES), F32)
    slab_even = slab % 2 == 0
    for position, out in enumerate(slab_outs):
        up = slab_even if position == 0 else jnp.logical_not(slab_even)
        out[:, 0:count] = jnp.where(up, high_first, low_first)
        out[0:16, count:] = jnp.where(up, coarse[:, LANES : 2 * LANES], coarse[:, 0:LANES])
        out[16:24, count:] = jnp.zeros((8, LANES), F32)
    for k in range(7):
        for half in range(2):
            row = 16 * k + 8 * half
            operator[row : row + 8] = jnp.concatenate(
                [operator_raw[k, 2 * half], operator_raw[k, 2 * half + 1]], axis=0
            )
    for copy in copies[6:]:
        copy.wait()


def fine_ghosts(rows, count, sizes, parity_in, cross_in, slab_ins):
    sub, slab = place()
    at = slice(0, count)
    slab_values = [ref[rows, at] for ref in slab_ins] + [None]
    below, above = neighbours(slab, sizes[1], slab_values[0], slab_values[1])
    left, right = neighbours(sub, sizes[0], parity_in[rows, at], cross_in[rows, at])
    return chunks_of(below) + chunks_of(above) + chunks_of(left) + chunks_of(right)


def apply_tile(table, operator, columns, at):
    total = None
    for k in range(7):
        near = twice(gather_four(table, columns[k : k + 1, at]))
        term = operator[16 * k : 16 * k + 16, at] * near
        total = term if total is None else total + term
    return sum_components(total)


def fine_second(
    sizes, source, operator, columns, sends, w_ref, first_ref, parity_in, cross_in, *rest
):
    slab_count = (len(rest) - 5) // 2
    slab_ins, rest = rest[:slab_count], rest[slab_count:]
    smoothed, parity_out, cross_out = rest[0], rest[1], rest[2]
    slab_outs, second_ref, picks = rest[3:-2], rest[-2], rest[-1]
    count = sends.shape[1] // 4
    ghosts = fine_ghosts(slice(0, 8), count, sizes, parity_in, cross_in, slab_ins)
    table = table_four(chunks_of(first_ref[...]) + ghosts)

    def step(at):
        residual = twice(source[:, at]) - apply_tile(table, operator, columns, at)
        second_ref[:, at] = first_ref[:, at] + residual / w_ref[:, at]

    tiles(source.shape[1], 1024, step)
    smoothed[...] = second_ref[0:4]
    table = table_four(chunks_of(second_ref[...]))

    def pick(at):
        picks[:, at] = gather_four(table, sends[:, at])

    tiles(sends.shape[1], 1024, pick)
    sub, slab = place()
    low_first, high_first = picks[:, 0:count], picks[:, count : 2 * count]
    low_second, high_second = picks[:, 2 * count : 3 * count], picks[:, 3 * count :]
    even = sub % 2 == 0
    parity_out[:, 0:count] = jnp.where(even, high_second, low_second)
    parity_out[:, count : count + LANES] = cross_in[0:8, count:]
    parity_out[:, count + LANES :] = cross_in[8:16, count:]
    cross_out[...] = jnp.where(even, low_second, high_second)
    slab_even = slab % 2 == 0
    for position, out in enumerate(slab_outs):
        up = slab_even if position == 0 else jnp.logical_not(slab_even)
        out[...] = jnp.where(up, high_first, low_first)


def coarsen(table, operator, prolong, columns, slots, aggregates, sums, count):
    tile = 512

    def step(at):
        wide_prolong = expand(prolong[:, at])
        totals = [[jnp.zeros((8, tile), F32) for _ in range(2)] for _ in range(7)]
        for k in range(7):
            column = columns[k : k + 1, at]
            near = choose_sixteen(matmul(table, onehot(column)), column >> 7)
            blocks = triple_product(wide_prolong, operator[16 * k : 16 * k + 16, at], near)
            slot = jnp.broadcast_to(slots[k : k + 1, at], (8, tile))
            for s in range(7):
                here = slot == s
                for half in range(2):
                    totals[s][half] = totals[s][half] + jnp.where(here, blocks[half], 0.0)
        for s in range(7):
            for half in range(2):
                row = 16 * s + 8 * half
                sums[row : row + 8, at] = totals[s][half]

    tiles(columns.shape[1], tile, step)
    return scatter(sums[...], aggregates[...], count)


def fine_coarsen(
    sizes, operator, prolong, columns, slots, aggregates, second_ref, parity_old, cross_old, *rest
):
    slab_old, (out, sums) = rest[:-2], rest[-2:]
    count = parity_old.shape[1]
    ghosts = fine_ghosts(slice(8, 24), count, sizes, parity_old, cross_old, slab_old)
    table = table_sixteen(chunks_of(prolong[...]) + ghosts)
    out[...] = coarsen(
        table, operator, prolong, columns, slots, aggregates, sums, out.shape[1]
    )


def fine_restrict(
    sizes,
    source,
    operator,
    prolong,
    columns,
    aggregates,
    second_ref,
    operator_own,
    parity_in,
    cross_in,
    *rest,
):
    slab_ins, (out, lifted) = rest[:-2], rest[-2:]
    ghosts = fine_ghosts(slice(0, 8), cross_in.shape[1], sizes, parity_in, cross_in, slab_ins)
    table = table_four(chunks_of(second_ref[...]) + ghosts)

    def step(at):
        residual = twice(source[:, at]) - apply_tile(table, operator, columns, at)
        lifted[:, at] = lift(prolong[:, at], residual)

    tiles(source.shape[1], 1024, step)
    out[0:112] = operator_own[...]
    out[112:120] = scatter(lifted[...], aggregates[...], out.shape[1])


def slab_faces(picks, slab, slab_outs):
    slab_even = slab % 2 == 0
    for position, out in enumerate(slab_outs):
        up = slab_even if position == 0 else jnp.logical_not(slab_even)
        out[...] = jnp.where(up, picks[:, LANES : 2 * LANES], picks[:, 0:LANES])


def pair_first(own, other, sends, operator, source, weights, first, group_out, *slab_outs):
    sub, slab = place()
    even = sub % 2 == 0
    half = own.shape[1]
    lower = jnp.where(even, own[...], other[...])
    upper = jnp.where(even, other[...], own[...])
    operator[:, 0:half] = lower[0:112]
    operator[:, half:] = upper[0:112]
    source[:, 0:half] = lower[112:120]
    source[:, half:] = upper[112:120]
    weights[...] = row_weights(lambda k: operator[16 * k : 16 * k + 16])
    first[...] = source[...] / weights[...]
    picks = gather_four(table_four(chunks_of(first[...])), sends[...])
    group_out[...] = picks[:, 2 * LANES :]
    slab_faces(picks, slab, slab_outs)


def pair_ghosts(sizes, even_in, odd_in, slab_ins):
    sub, slab = place()
    values = [ref[...] for ref in slab_ins] + [None]
    below, above = neighbours(slab, sizes[1], values[0], values[1])
    left, right = neighbours(sub // 2, sizes[0] // 2, even_in[...], odd_in[...])
    return [below, above, swap_halves(left, right, LANES // 2)]


def pair_second(
    sizes, operator, source, weights, first, columns, sends, even_in, odd_in, *rest
):
    slab_count = (len(rest) - 3) // 2
    slab_ins, rest = rest[:slab_count], rest[slab_count:]
    smoothed, second_ref, group_out = rest[0], rest[1], rest[2]
    slab_outs = rest[3:]
    table = table_four(chunks_of(first[...]) + pair_ghosts(sizes, even_in, odd_in, slab_ins))

    def step(at):
        residual = source[:, at] - apply_tile(table, operator, columns, at)
        second_ref[:, at] = first[:, at] + residual / weights[:, at]

    tiles(source.shape[1], 512, step)
    sub, slab = place()
    half = smoothed.shape[1]
    smoothed[...] = jnp.where(sub % 2 == 0, second_ref[0:4, 0:half], second_ref[0:4, half:])
    picks = gather_four(table_four(chunks_of(second_ref[...])), sends[...])
    group_out[...] = picks[:, 2 * LANES :]
    slab_faces(picks, slab, slab_outs)


def pair_coarsen(
    sizes,
    operator,
    prolong,
    columns,
    slots,
    aggregates,
    parity_old,
    cross_old,
    forwarded,
    *rest,
):
    slab_old, (operator_two, weights_two, sums) = rest[:-3], rest[-3:]
    sub, slab = place()
    even = sub % 2 == 0
    count = parity_old.shape[1]
    values = [ref[0:16, count:] for ref in slab_old] + [None]
    below, above = neighbours(slab, sizes[1], values[0], values[1])
    mine = cross_old[0:16, count:]
    partners = jnp.concatenate(
        [forwarded[:, count : count + LANES], forwarded[:, count + LANES :]], axis=0
    )
    group = sub // 2
    left = jnp.where(even, mine, partners)
    right = jnp.where(even, partners, mine)
    left = jnp.where(group > 0, left, jnp.zeros_like(left))
    right = jnp.where(group < sizes[0] // 2 - 1, right, jnp.zeros_like(right))
    ghosts = [below, above, swap_halves(left, right, LANES // 2)]
    table = table_sixteen(chunks_of(prolong[...]) + ghosts)
    operator_two[...] = coarsen(
        table, operator, prolong, columns, slots, aggregates, sums, LANES
    )
    weights_two[...] = row_weights(lambda k: operator_two[16 * k : 16 * k + 16])


def pair_restrict(
    sizes,
    operator,
    source,
    second_ref,
    prolong,
    columns,
    aggregates,
    sends,
    weights_two,
    even_in,
    odd_in,
    *rest,
):
    slab_count = (len(rest) - 4) // 2
    slab_ins, rest = rest[:slab_count], rest[slab_count:]
    source_two, first_two, whole_out = rest[:3]
    slab_outs, lifted = rest[3:-1], rest[-1]
    sub, slab = place()
    table = table_four(chunks_of(second_ref[...]) + pair_ghosts(sizes, even_in, odd_in, slab_ins))

    def step(at):
        residual = source[:, at] - apply_tile(table, operator, columns, at)
        lifted[:, at] = lift(prolong[:, at], residual)

    tiles(source.shape[1], 512, step)
    total = scatter(lifted[...], aggregates[...], LANES)
    source_two[...] = total
    first = total / weights_two[...]
    first_two[...] = first
    half = LANES // 2
    lane = lax.broadcasted_iota(jnp.int32, first.shape, 1)
    first = jnp.where(lane < half, first, 0.0)
    placed = jnp.where(sub // 2 % 2 == 0, first, pltpu.roll(first, half, 1))
    filler = jnp.zeros((1, -sends.shape[1] % LANES), jnp.int32)
    picks = gather_four(table_four([placed]), jnp.concatenate([sends[...], filler], axis=1))
    faces = picks[:, 0:LANES]
    seconds = pltpu.roll(picks[:, LANES:], half, 1)

    def sent(value):
        return jnp.where(lane < half, value, seconds)

    whole_out[...] = sent(first)
    slab_even = slab % 2 == 0
    for position, out in enumerate(slab_outs):
        up = slab_even if position == 0 else jnp.logical_not(slab_even)
        out[...] = sent(jnp.where(up, pltpu.roll(faces, half, 1), faces))


def group_apply(sizes, operator, first_two, columns, *rest):
    received, out = rest[:-1], rest[-1]
    sub, slab = place()
    group, pair = sub // 4, sub // 2 % 2
    even = sub % 2 == 0
    half = LANES // 2
    lane = lax.broadcasted_iota(jnp.int32, (8, LANES), 1)
    none = jnp.zeros((8, LANES), F32)

    def left_part(value):
        return jnp.where(lane < half, value, 0.0)

    mine, other = left_part(first_two[...]), left_part(received[0][...])
    first = jnp.where(
        pair == 0, mine + pltpu.roll(other, half, 1), other + pltpu.roll(mine, half, 1)
    )
    first = jnp.where(even, first, none)

    odd = received[3][...] + received[4][...] if len(received) > 4 else None
    below, above = neighbours(slab, sizes[1], received[1][...] + received[2][...], odd)
    firsts = jnp.where(even, left_part(below) + pltpu.roll(left_part(above), half, 1), none)

    left, right = neighbours(
        group,
        sizes[0] // 4,
        received[0][...] + received[2][...],
        received[1][...] + received[3][...],
    )
    width = GX // 4 * (GZ // 4)
    left = pltpu.roll(left, LANES - half - width, 1)
    right = pltpu.roll(right, LANES - half + width, 1)
    seconds = jnp.where(lane < width, left, jnp.where(lane < 2 * width, right, 0.0))
    seconds = jnp.where(even, none, seconds)

    table = table_four([first, firsts, seconds])
    mine = jnp.where(pair == 0, columns[...], pltpu.roll(columns[...], half, 1))
    total = None
    for k in range(7):
        near = twice(gather_four(table, mine[k : k + 1]))
        term = operator[16 * k : 16 * k + 16] * near
        total = term if total is None else total + term
    out[...] = sum_components(total)


def group_second(source, weights, first_two, own, other, out):
    sub, slab = place()
    residual = source[...] - (own[...] + other[...])
    second = first_two[...] + residual / weights[...]
    share = out.shape[1]
    out[...] = jnp.where(sub % 2 == 0, second[0:4, 0:share], second[0:4, share : 2 * share])


def swap_by_core(value, even_mate, odd_mate):
    subs, slabs = lax.axis_size("sub"), lax.axis_size("slab")
    route = []
    for sub in range(subs):
        for slab in range(slabs):
            target = (even_mate if sub % 2 == 0 else odd_mate)(sub, slab)
            if not (0 <= target[0] < subs and 0 <= target[1] < slabs):
                target = (sub ^ 2, slab)
            route.append((sub * slabs + slab, target[0] * slabs + target[1]))
    return lax.ppermute(value, ("sub", "slab"), route)


def odd_mate_of(index):
    return ((index - 1) ^ 1) + 1


def group_exchange(whole, slab_values):
    def along_sub(odd, flip):
        def mate(sub, slab):
            block = odd_mate_of(sub // 4) if odd else sub // 4 ^ 1
            return block * 4 + (sub % 4 ^ flip), slab

        return mate

    def along_slab(odd, flip):
        return lambda sub, slab: (sub ^ flip, odd_mate_of(slab) if odd else slab ^ 1)

    def pair(sub, slab):
        return sub ^ 2, slab

    first = slab_values[0]
    received = [
        swap_by_core(whole, pair, along_sub(False, 0)),
        swap_by_core(first, along_slab(False, 0), along_sub(True, 0)),
        swap_by_core(first, along_slab(False, 2), along_sub(False, 2)),
    ]
    if len(slab_values) == 1:
        return received + [swap_by_core(first, pair, along_sub(True, 2))]
    second = slab_values[1]
    return received + [
        swap_by_core(second, along_slab(True, 0), along_sub(True, 2)),
        swap_by_core(second, along_slab(True, 2), pair),
    ]


def sub_pairing(value, group, odd):
    subs, slabs = lax.axis_size("sub"), lax.axis_size("slab")
    route = []
    for sub in range(subs):
        block = sub // group
        mate = ((block - 1) ^ 1) + 1 if odd else block ^ 1
        for slab in range(slabs):
            target = (mate * group + sub % group, slab)
            if not 0 <= mate < subs // group:
                target = (sub ^ group // 2, slab) if group > 1 else (sub, slab ^ 1)
            route.append((sub * slabs + slab, target[0] * slabs + target[1]))
    return lax.ppermute(value, ("sub", "slab"), route)


def slab_pairing(value, odd):
    subs, slabs = lax.axis_size("sub"), lax.axis_size("slab")
    route = []
    for sub in range(subs):
        for slab in range(slabs):
            mate = ((slab - 1) ^ 1) + 1 if odd else slab ^ 1
            target = (sub, mate) if 0 <= mate < slabs else (sub ^ 1, slab)
            route.append((sub * slabs + slab, target[0] * slabs + target[1]))
    return lax.ppermute(value, ("sub", "slab"), route)


def slab_pairings(values):
    return [slab_pairing(value, position == 1) for position, value in enumerate(values)]


def on_device(
    source,
    operator,
    prolong,
    columns,
    slots,
    aggregates,
    sends,
    prolong_one,
    columns_one,
    slots_one,
    aggregates_one,
    sends_one,
    columns_two,
    sends_two,
):
    sizes = (lax.axis_size("sub"), lax.axis_size("slab"))
    slab_moves = 1 if sizes[1] == 2 else 2
    rows = source.shape[1]
    rows_one = rows // 8
    pair_rows_one = 2 * rows_one
    count = 2 * GY * GZ
    kept = [
        source,
        sends,
        sends_one,
        columns,
        slots,
        aggregates,
        columns_one,
        slots_one,
        aggregates_one,
        columns_two,
        sends_two,
    ]
    raw = [operator, kept[0], prolong, kept[1], prolong_one, kept[2], *kept[3:]]
    handed = len(kept)
    out = call(
        functools.partial(fine_first, handed, slab_moves),
        [((1, value.shape[0]) if value.ndim == 1 else value.shape, value.dtype) for value in kept]
        + [(112, rows), (16, rows), (16, pair_rows_one)]
        + [(8, rows), (8, rows), (24, count), (24, count + LANES)]
        + [(24, count + LANES)] * slab_moves,
        *[pltpu.with_memory_space_constraint(value, pltpu.HBM) for value in raw],
        scratch=[
            pltpu.VMEM(operator.shape, F32),
            pltpu.VMEM(prolong.shape, F32),
            pltpu.VMEM(prolong_one.shape, F32),
            pltpu.VMEM((24, rows), F32),
            pltpu.SemaphoreType.DMA((len(raw),)),
        ],
        space=pltpu.HBM,
    )
    source, sends, sends_one, columns, slots, aggregates = out[:6]
    columns_one, slots_one, aggregates_one, columns_two, sends_two = out[6:11]
    operator, prolong, prolong_one, weights, first, even, odd, *slabs = out[11:]
    even_old = sub_pairing(even, 1, False)
    odd_old = sub_pairing(odd, 1, True)
    slabs_old = slab_pairings(slabs)

    smoothed, even, odd, *rest = call(
        functools.partial(fine_second, sizes),
        [(4, rows), (8, count + 2 * LANES), (8, count)]
        + [(8, count)] * slab_moves
        + [(8, rows)],
        source,
        operator,
        columns,
        sends,
        weights,
        first,
        even_old,
        odd_old,
        *slabs_old,
        scratch=[pltpu.VMEM((8, sends.shape[1]), F32)],
    )
    slabs, second = rest[:-1], rest[-1]
    forwarded = sub_pairing(even, 1, False)
    odd_in = sub_pairing(odd, 1, True)
    slabs_in = slab_pairings(slabs)

    (operator_own,) = call(
        functools.partial(fine_coarsen, sizes),
        [(112, rows_one)],
        operator,
        prolong,
        columns,
        slots,
        aggregates,
        second,
        even_old,
        odd_old,
        *slabs_old,
        scratch=[pltpu.VMEM((112, rows), F32)],
        flops=4 * 10**9,
    )
    (own,) = call(
        functools.partial(fine_restrict, sizes),
        [(120, rows_one)],
        source,
        operator,
        prolong,
        columns,
        aggregates,
        second,
        operator_own,
        forwarded,
        odd_in,
        *slabs_in,
        scratch=[pltpu.VMEM((8, rows), F32)],
    )
    other = sub_pairing(own, 1, False)

    faces = [(8, LANES)] * (1 + slab_moves)
    operator_one, source_one, weights_one, first_one, group_out, *slabs = call(
        pair_first,
        [(112, pair_rows_one)] + [(8, pair_rows_one)] * 3 + faces,
        own,
        other,
        sends_one,
    )
    even_in = sub_pairing(group_out, 2, False)
    odd_in = sub_pairing(group_out, 2, True)
    slabs_in = slab_pairings(slabs)

    operator_two, weights_two = call(
        functools.partial(pair_coarsen, sizes),
        [(112, LANES), (8, LANES)],
        operator_one,
        prolong_one,
        columns_one,
        slots_one,
        aggregates_one,
        even_old,
        odd_old,
        forwarded,
        *slabs_old,
        scratch=[pltpu.VMEM((112, pair_rows_one), F32)],
        flops=10**9,
    )
    smoothed_one, second_one, group_out, *slabs = call(
        functools.partial(pair_second, sizes),
        [(4, rows_one), (8, pair_rows_one)] + faces,
        operator_one,
        source_one,
        weights_one,
        first_one,
        columns_one,
        sends_one,
        even_in,
        odd_in,
        *slabs_in,
    )
    even_in = sub_pairing(group_out, 2, False)
    odd_in = sub_pairing(group_out, 2, True)
    slabs_in = slab_pairings(slabs)

    source_two, first_two, whole, *slabs = call(
        functools.partial(pair_restrict, sizes),
        [(8, LANES), (8, LANES)] + faces,
        operator_one,
        source_one,
        second_one,
        prolong_one,
        columns_one,
        aggregates_one,
        sends_two,
        weights_two,
        even_in,
        odd_in,
        *slabs_in,
        scratch=[pltpu.VMEM((8, pair_rows_one), F32)],
    )
    received = group_exchange(whole, slabs)
    (applied,) = call(
        functools.partial(group_apply, sizes),
        [(8, LANES)],
        operator_two,
        first_two,
        columns_two,
        *received,
    )
    applied_other = sub_pairing(applied, 1, False)
    (smoothed_two,) = call(
        group_second,
        [(4, rows_one // 8)],
        source_two,
        weights_two,
        first_two,
        applied,
        applied_other,
    )
    return (smoothed, smoothed_one, smoothed_two)


def solution(mesh):
    placed = (
        P(None, ("sub", "slab")),
        P(None, None, None, ("sub", "slab")),
        P(None, None, ("sub", "slab")),
        P(None, ("sub", "slab")),
        P(None, ("sub", "slab")),
        P(("sub", "slab")),
        P(("sub", "slab")),
        P(None, None, ("sub", "slab")),
        P(None, ("sub", "slab")),
        P(None, ("sub", "slab")),
        P(("sub", "slab")),
        P(("sub", "slab")),
        P(None, ("sub", "slab")),
        P(("sub", "slab")),
    )
    return jax.shard_map(
        on_device,
        mesh=mesh,
        in_specs=placed,
        out_specs=(P(None, ("sub", "slab")), P(None, ("sub", "slab")), P(None, ("sub", "slab"))),
        check_vma=False,
    )
```

```python
import functools

import jax
import jax.numpy as jnp
from jax import lax
from jax.experimental import pallas as pl
from jax.experimental.pallas import tpu as pltpu
from jax.sharding import PartitionSpec as P

GX = 8
GY = 8
GZ = 32
LANES = 128
OWN_SLOTS = 7
FINE_FIRST = (0, 1, 2)
FINE_SECOND = (0, 1, 2)
PAIR_FIRST = (0, 1, 2)
PAIR_SECOND = (0, 1, 2)
GROUP = (0, 3, 2, 1)


def ordered(values, order):
    return [values[at] for at in order] + list(values[len(order) :])


def restored(refs, order):
    return [refs[order.index(at)] for at in range(len(order))] + list(refs[len(order) :])
F32 = jnp.float32
BF16 = jnp.bfloat16


def split(value):
    high = value.astype(BF16)
    return high, (value - high.astype(F32)).astype(BF16)


def upper_half(shape):
    return lax.broadcasted_iota(jnp.int32, shape, 0) >= 4


def fold(value):
    return value + pltpu.roll(value, 4, 0)


def pair_rows(first, second):
    return jnp.where(upper_half(first.shape), second, first)


def twice(rows):
    return jnp.concatenate([rows, rows], axis=0)


def table_four(chunks):
    if len(chunks) % 2:
        chunks = chunks + [jnp.zeros_like(chunks[0])]
    rows = [pair_rows(chunks[j], chunks[j + 1]) for j in range(0, len(chunks), 2)]
    return jnp.concatenate(split(jnp.concatenate(rows, axis=0)), axis=1)


def table_sixteen(chunks):
    return jnp.concatenate(split(jnp.concatenate(chunks, axis=0)), axis=1)


def onehot(columns):
    low = (columns & (LANES - 1)).astype(jnp.int16)
    low = jnp.broadcast_to(low, (LANES, columns.shape[1]))
    here = lax.broadcasted_iota(jnp.int16, low.shape, 0) == low
    return twice(jnp.where(here, jnp.ones((), BF16), jnp.zeros((), BF16)))


def choose_four(picked, high):
    shape = (8, picked.shape[1])
    high = jnp.broadcast_to(high, shape) - upper_half(shape).astype(jnp.int32)
    total = jnp.zeros(shape, F32)
    for j in range(picked.shape[0] // 8):
        total = jnp.where(high == 2 * j, picked[8 * j : 8 * j + 8], total)
    return fold(total)


def choose_sixteen(picked, high):
    shape = (8, picked.shape[1])
    high = jnp.broadcast_to(high, shape)
    total = [jnp.zeros(shape, F32), jnp.zeros(shape, F32)]
    for j in range(picked.shape[0] // 16):
        here = high == j
        for half in range(2):
            at = 16 * j + 8 * half
            total[half] = jnp.where(here, picked[at : at + 8], total[half])
    return total


def matmul(left, right):
    return jnp.dot(left, right, preferred_element_type=F32)


def gather_four(table, columns):
    return choose_four(matmul(table, onehot(columns)), columns >> 7)


def gather_halves(table, columns, chunk):
    return choose_sixteen(matmul(table, onehot(columns)), (columns >> 7) - chunk)


def gather_sixteen(table, columns):
    return jnp.concatenate(gather_halves(table, columns, 0), axis=0)


def sum_components(value):
    first = value.astype(BF16)
    rest = value - first.astype(F32)
    second = rest.astype(BF16)
    third = (rest - second.astype(F32)).astype(BF16)
    row = lax.broadcasted_iota(jnp.int32, (8, 48), 0) & 3
    column = (lax.broadcasted_iota(jnp.int32, (8, 48), 1) >> 2) & 3
    ones = (row == column).astype(F32).astype(BF16)
    return matmul(ones, jnp.concatenate([first, second, third], axis=0))


def row_weights(operator_at):
    total = jnp.abs(operator_at(0))
    for k in range(1, 7):
        total = total + jnp.abs(operator_at(k))
    return 1.0 + sum_components(total)


def spread_row(value, row, rows=8):
    return jnp.broadcast_to(value[row : row + 1], (rows, value.shape[1]))


def lift(prolong, residual):
    low = pair_rows(spread_row(residual, 0), spread_row(residual, 1))
    high = pair_rows(spread_row(residual, 2), spread_row(residual, 3))
    return fold(prolong[:8] * low + prolong[8:] * high)


def expand(rows):
    return [
        [pair_rows(spread_row(rows, 4 * a + 2 * h), spread_row(rows, 4 * a + 2 * h + 1)) for h in (0, 1)]
        for a in range(4)
    ]


def triple_product(wide_prolong, operator, near):
    wide = expand(operator)
    out = [None, None]
    for a in range(4):
        inner = fold(wide[a][0] * near[0] + wide[a][1] * near[1])
        for half in range(2):
            term = wide_prolong[a][half] * inner
            out[half] = term if out[half] is None else out[half] + term
    return out


def scatter(values, targets, count):
    high, low = split(values)
    shape = (count, values.shape[1])
    hot = lax.broadcasted_iota(jnp.int32, shape, 0) == jnp.broadcast_to(targets, shape)
    hot = hot.astype(F32).astype(BF16)
    both = lax.dot_general(
        jnp.concatenate([high, low], axis=0),
        hot,
        (((1,), (1,)), ((), ())),
        preferred_element_type=F32,
    )
    rows = values.shape[0]
    return both[:rows] + both[rows:]


def chunks_of(value):
    return [value[:, at : at + LANES] for at in range(0, value.shape[1], LANES)]


def place():
    sub, slab = lax.axis_index("sub"), lax.axis_index("slab")
    return sub, slab


def neighbours(index, count, even, odd):
    is_even = index % 2 == 0
    if odd is None:
        odd = jnp.zeros_like(even)
    below = jnp.where(is_even, odd, even)
    above = jnp.where(is_even, even, odd)
    below = jnp.where(index > 0, below, jnp.zeros_like(below))
    above = jnp.where(index < count - 1, above, jnp.zeros_like(above))
    return below, above


def swap_halves(below, above, half):
    lane = lax.broadcasted_iota(jnp.int32, below.shape, 1)
    return pltpu.roll(jnp.where(lane < half, above, below), half, 1)


def call(body, outs, *args, scratch=(), flops=0, space=pltpu.VMEM):
    outs = [(out, F32) if isinstance(out[0], int) else out for out in outs]
    cost = pl.CostEstimate(flops=flops, bytes_accessed=0, transcendentals=0) if flops else None
    return pl.pallas_call(
        body,
        out_shape=[jax.ShapeDtypeStruct(shape, dtype) for shape, dtype in outs],
        in_specs=[pl.BlockSpec(memory_space=space)] * len(args),
        out_specs=[pl.BlockSpec(memory_space=pltpu.VMEM)] * len(outs),
        scratch_shapes=list(scratch),
        cost_estimate=cost,
        compiler_params=pltpu.CompilerParams(vmem_limit_bytes=32 * 1024 * 1024),
    )(*args)


def tiles(count, tile, body):
    def step(index, carry):
        body(pl.ds(pl.multiple_of(index * tile, tile), tile))
        return carry

    lax.fori_loop(0, count // tile, step, 0, unroll=True)


def fine_first(handed, slab_moves, *refs):
    count = handed + 3
    raw, refs = refs[:count], refs[count:]
    kept, refs = refs[:handed], refs[handed:]
    operator_raw, prolong, prolong_one, w_ref, first_ref, parity_out, cross_out = refs[:7]
    slab_outs, refs = refs[7 : 7 + slab_moves], refs[7 + slab_moves :]
    prolong_raw, prolong_one_raw, picks, semaphores, slot_semaphores = refs
    source, sends, sends_one = kept[0], kept[1], kept[2]
    targets = [source, prolong_raw, sends, prolong_one_raw, sends_one, *kept[3:]]
    slot_copies = [
        pltpu.make_async_copy(raw[0].at[k], operator_raw.at[k], slot_semaphores.at[k])
        for k in range(7)
    ]
    copies = [
        pltpu.make_async_copy(
            value, target if value.ndim > 1 else target.at[0], semaphores.at[at]
        )
        for at, (value, target) in enumerate(zip(raw[1:], targets))
    ]
    for copy in slot_copies + copies:
        copy.start()
    sums = [None] * 4
    for k in range(7):
        slot_copies[k].wait()
        for a in range(4):
            value = jnp.abs(operator_raw[k, a])
            sums[a] = value if sums[a] is None else sums[a] + value
    weights = 1.0 + sum_components(jnp.concatenate(sums, axis=0))
    copies[0].wait()
    first = twice(source[...]) / weights
    w_ref[...] = weights
    first_ref[...] = first
    for at in range(1, 5):
        copies[at].wait()
    for half in range(2):
        at = slice(8 * half, 8 * half + 8)
        prolong[at] = jnp.concatenate([prolong_raw[2 * half], prolong_raw[2 * half + 1]], axis=0)
        prolong_one[at] = jnp.concatenate(
            [prolong_one_raw[2 * half], prolong_one_raw[2 * half + 1]], axis=0
        )
    table = jnp.concatenate(
        [table_four(chunks_of(first)), table_sixteen(chunks_of(prolong[...]))], axis=0
    )
    split_at = first.shape[1] // LANES * 4

    def pick(at):
        columns = sends[:, at]
        picked = matmul(table, onehot(columns))
        picks[0:8, at] = choose_four(picked[:split_at], columns >> 7)
        low, high = choose_sixteen(picked[split_at:], columns >> 7)
        picks[8:16, at] = low
        picks[16:24, at] = high

    tiles(sends.shape[1], 512, pick)
    coarse = gather_sixteen(table_sixteen(chunks_of(prolong_one[...])), sends_one[...])
    sub, slab = place()
    count = sends.shape[1] // 4
    low_first, high_first = picks[:, 0:count], picks[:, count : 2 * count]
    low_second, high_second = picks[:, 2 * count : 3 * count], picks[:, 3 * count :]
    even = sub % 2 == 0
    parity_out[...] = jnp.where(even, high_second, low_second)
    cross_out[:, 0:count] = jnp.where(even, low_second, high_second)
    cross_out[0:16, count:] = coarse[:, 2 * LANES :]
    cross_out[16:24, count:] = jnp.zeros((8, LANES), F32)
    slab_even = slab % 2 == 0
    for position, out in enumerate(slab_outs):
        up = slab_even if position == 0 else jnp.logical_not(slab_even)
        out[:, 0:count] = jnp.where(up, high_first, low_first)
        out[0:16, count:] = jnp.where(up, coarse[:, LANES : 2 * LANES], coarse[:, 0:LANES])
        out[16:24, count:] = jnp.zeros((8, LANES), F32)
    for copy in copies[5:]:
        copy.wait()


def fine_own(operator_raw, prolong, columns, operator, own_near):
    table = table_sixteen(chunks_of(prolong[...]))

    def step(at):
        for k in range(own_near.shape[0] // 16):
            low, high = gather_halves(table, columns[k : k + 1, at], 0)
            own_near[16 * k : 16 * k + 8, at] = low
            own_near[16 * k + 8 : 16 * k + 16, at] = high

    tiles(columns.shape[1], 512, step)
    for k in range(7):
        for half in range(2):
            row = 16 * k + 8 * half
            operator[row : row + 8] = jnp.concatenate(
                [operator_raw[k, 2 * half], operator_raw[k, 2 * half + 1]], axis=0
            )


def fine_ghosts(rows, count, sizes, parity_in, cross_in, slab_ins):
    sub, slab = place()
    at = slice(0, count)
    slab_values = [ref[rows, at] for ref in slab_ins] + [None]
    below, above = neighbours(slab, sizes[1], slab_values[0], slab_values[1])
    left, right = neighbours(sub, sizes[0], parity_in[rows, at], cross_in[rows, at])
    return chunks_of(below) + chunks_of(above) + chunks_of(left) + chunks_of(right)


def apply_tile(table, operator, columns, at):
    total = None
    for k in range(7):
        near = twice(gather_four(table, columns[k : k + 1, at]))
        term = operator[16 * k : 16 * k + 16, at] * near
        total = term if total is None else total + term
    return sum_components(total)


def fine_second(
    sizes, source, operator, columns, sends, w_ref, first_ref, *rest
):
    slab_count = (len(rest) - 6) // 2
    taken, rest = restored(rest[: slab_count + 2], FINE_FIRST), rest[slab_count + 2 :]
    parity_in, cross_in, *slab_ins = taken
    parity_out, cross_out = rest[0], rest[1]
    slab_outs, second_ref, picks = rest[2:-2], rest[-2], rest[-1]
    count = sends.shape[1] // 4
    ghosts = fine_ghosts(slice(0, 8), count, sizes, parity_in, cross_in, slab_ins)
    table = table_four(chunks_of(first_ref[...]) + ghosts)

    def step(at):
        residual = twice(source[:, at]) - apply_tile(table, operator, columns, at)
        second_ref[:, at] = first_ref[:, at] + residual / w_ref[:, at]

    tiles(source.shape[1], 1024, step)
    table = table_four(chunks_of(second_ref[...]))

    def pick(at):
        picks[:, at] = gather_four(table, sends[:, at])

    tiles(sends.shape[1], 1024, pick)
    sub, slab = place()
    low_first, high_first = picks[:, 0:count], picks[:, count : 2 * count]
    low_second, high_second = picks[:, 2 * count : 3 * count], picks[:, 3 * count :]
    even = sub % 2 == 0
    parity_out[:, 0:count] = jnp.where(even, high_second, low_second)
    parity_out[:, count : count + LANES] = cross_in[0:8, count:]
    parity_out[:, count + LANES :] = cross_in[8:16, count:]
    cross_out[...] = jnp.where(even, low_second, high_second)
    slab_even = slab % 2 == 0
    for position, out in enumerate(slab_outs):
        up = slab_even if position == 0 else jnp.logical_not(slab_even)
        out[...] = jnp.where(up, high_first, low_first)


def coarsen(tables, operator, prolong, columns, slots, aggregates, sums, count, own_near=None):
    tile = 512
    whole = jnp.concatenate(tables, axis=0)
    known = 0 if own_near is None else own_near.shape[0] // 16

    def step(at):
        wide_prolong = expand(prolong[:, at])
        totals = [[jnp.zeros((8, tile), F32) for _ in range(2)] for _ in range(7)]
        for k in range(7):
            column = columns[k : k + 1, at]
            if k < known:
                near = gather_halves(tables[1], column, tables[0].shape[0] // 16)
                near = [
                    near[half] + own_near[16 * k + 8 * half : 16 * k + 8 * half + 8, at]
                    for half in range(2)
                ]
            else:
                near = gather_halves(whole, column, 0)
            blocks = triple_product(wide_prolong, operator[16 * k : 16 * k + 16, at], near)
            slot = jnp.broadcast_to(slots[k : k + 1, at], (8, tile))
            for s in range(7):
                here = slot == s
                for half in range(2):
                    totals[s][half] = totals[s][half] + jnp.where(here, blocks[half], 0.0)
        for s in range(7):
            for half in range(2):
                row = 16 * s + 8 * half
                sums[row : row + 8, at] = totals[s][half]

    tiles(columns.shape[1], tile, step)
    return scatter(sums[...], aggregates[...], count)


def fine_coarsen(
    sizes,
    operator,
    prolong,
    columns,
    slots,
    aggregates,
    own_near,
    second_ref,
    parity_old,
    cross_old,
    *rest,
):
    slab_old, (out, sums) = rest[:-2], rest[-2:]
    count = parity_old.shape[1]
    ghosts = fine_ghosts(slice(8, 24), count, sizes, parity_old, cross_old, slab_old)
    tables = [table_sixteen(chunks_of(prolong[...])), table_sixteen(ghosts)]
    out[...] = coarsen(
        tables, operator, prolong, columns, slots, aggregates, sums, out.shape[1], own_near
    )


def fine_restrict(
    sizes,
    source,
    operator,
    prolong,
    columns,
    aggregates,
    second_ref,
    operator_own,
    *rest,
):
    parity_in, cross_in, *slab_ins = restored(rest[:-2], FINE_SECOND)
    out, lifted = rest[-2:]
    ghosts = fine_ghosts(slice(0, 8), cross_in.shape[1], sizes, parity_in, cross_in, slab_ins)
    table = table_four(chunks_of(second_ref[...]) + ghosts)

    def step(at):
        residual = twice(source[:, at]) - apply_tile(table, operator, columns, at)
        lifted[:, at] = lift(prolong[:, at], residual)

    tiles(source.shape[1], 1024, step)
    out[0:112] = operator_own[...]
    out[112:120] = scatter(lifted[...], aggregates[...], out.shape[1])


def slab_faces(picks, slab, slab_outs):
    slab_even = slab % 2 == 0
    for position, out in enumerate(slab_outs):
        up = slab_even if position == 0 else jnp.logical_not(slab_even)
        out[...] = jnp.where(up, picks[:, LANES : 2 * LANES], picks[:, 0:LANES])


def pair_first(own, other, sends, operator, source, weights, first, group_out, *slab_outs):
    sub, slab = place()
    even = sub % 2 == 0
    half = own.shape[1]
    lower = jnp.where(even, own[...], other[...])
    upper = jnp.where(even, other[...], own[...])
    operator[:, 0:half] = lower[0:112]
    operator[:, half:] = upper[0:112]
    source[:, 0:half] = lower[112:120]
    source[:, half:] = upper[112:120]
    weights[...] = row_weights(lambda k: operator[16 * k : 16 * k + 16])
    first[...] = source[...] / weights[...]
    picks = gather_four(table_four(chunks_of(first[...])), sends[...])
    group_out[...] = picks[:, 2 * LANES :]
    slab_faces(picks, slab, slab_outs)


def pair_ghosts(sizes, even_in, odd_in, slab_ins):
    sub, slab = place()
    values = [ref[...] for ref in slab_ins] + [None]
    below, above = neighbours(slab, sizes[1], values[0], values[1])
    left, right = neighbours(sub // 2, sizes[0] // 2, even_in[...], odd_in[...])
    return [below, above, swap_halves(left, right, LANES // 2)]


def pair_second(
    sizes, operator, source, weights, first, columns, sends, *rest
):
    slab_count = (len(rest) - 4) // 2
    taken, rest = restored(rest[: slab_count + 2], PAIR_FIRST), rest[slab_count + 2 :]
    even_in, odd_in, *slab_ins = taken
    second_ref, group_out = rest[0], rest[1]
    slab_outs = rest[2:]
    table = table_four(chunks_of(first[...]) + pair_ghosts(sizes, even_in, odd_in, slab_ins))

    def step(at):
        residual = source[:, at] - apply_tile(table, operator, columns, at)
        second_ref[:, at] = first[:, at] + residual / weights[:, at]

    tiles(source.shape[1], 512, step)
    sub, slab = place()
    picks = gather_four(table_four(chunks_of(second_ref[...])), sends[...])
    group_out[...] = picks[:, 2 * LANES :]
    slab_faces(picks, slab, slab_outs)


def pair_coarsen(
    sizes,
    operator,
    prolong,
    columns,
    slots,
    aggregates,
    second_fine,
    second_ref,
    parity_old,
    cross_old,
    forwarded,
    *rest,
):
    slab_old, rest = rest[:-5], rest[-5:]
    operator_two, weights_two, smoothed, smoothed_one, sums = rest
    sub, slab = place()
    even = sub % 2 == 0
    half = smoothed_one.shape[1]
    smoothed[...] = second_fine[0:4]
    smoothed_one[...] = jnp.where(even, second_ref[0:4, 0:half], second_ref[0:4, half:])
    count = parity_old.shape[1]
    values = [ref[0:16, count:] for ref in slab_old] + [None]
    below, above = neighbours(slab, sizes[1], values[0], values[1])
    mine = cross_old[0:16, count:]
    partners = jnp.concatenate(
        [forwarded[:, count : count + LANES], forwarded[:, count + LANES :]], axis=0
    )
    group = sub // 2
    left = jnp.where(even, mine, partners)
    right = jnp.where(even, partners, mine)
    left = jnp.where(group > 0, left, jnp.zeros_like(left))
    right = jnp.where(group < sizes[0] // 2 - 1, right, jnp.zeros_like(right))
    ghosts = [below, above, swap_halves(left, right, LANES // 2)]
    tables = [table_sixteen(chunks_of(prolong[...])), table_sixteen(ghosts)]
    operator_two[...] = coarsen(
        tables, operator, prolong, columns, slots, aggregates, sums, LANES
    )
    weights_two[...] = row_weights(lambda k: operator_two[16 * k : 16 * k + 16])


def pair_restrict(
    sizes,
    operator,
    source,
    second_ref,
    prolong,
    columns,
    aggregates,
    sends,
    weights_two,
    *rest,
):
    slab_count = (len(rest) - 6) // 2
    taken, rest = restored(rest[: slab_count + 2], PAIR_SECOND), rest[slab_count + 2 :]
    even_in, odd_in, *slab_ins = taken
    source_two, first_two, whole_out = rest[:3]
    slab_outs, lifted = rest[3:-1], rest[-1]
    sub, slab = place()
    table = table_four(chunks_of(second_ref[...]) + pair_ghosts(sizes, even_in, odd_in, slab_ins))

    def step(at):
        residual = source[:, at] - apply_tile(table, operator, columns, at)
        lifted[:, at] = lift(prolong[:, at], residual)

    tiles(source.shape[1], 512, step)
    total = scatter(lifted[...], aggregates[...], LANES)
    source_two[...] = total
    first = total / weights_two[...]
    first_two[...] = first
    half = LANES // 2
    lane = lax.broadcasted_iota(jnp.int32, first.shape, 1)
    first = jnp.where(lane < half, first, 0.0)
    placed = jnp.where(sub // 2 % 2 == 0, first, pltpu.roll(first, half, 1))
    filler = jnp.zeros((1, -sends.shape[1] % LANES), jnp.int32)
    picks = gather_four(table_four([placed]), jnp.concatenate([sends[...], filler], axis=1))
    faces = picks[:, 0:LANES]
    seconds = pltpu.roll(picks[:, LANES:], half, 1)

    def sent(value):
        return jnp.where(lane < half, value, seconds)

    slab_even = slab % 2 == 0
    for position, out in enumerate(slab_outs):
        up = slab_even if position == 0 else jnp.logical_not(slab_even)
        out[...] = sent(jnp.where(up, pltpu.roll(faces, half, 1), faces))
    whole_out[...] = jnp.where(sub % 2 == 0, sent(first), slab_outs[0][...])


def group_apply(sizes, operator, first_two, columns, *rest):
    received, out = restored(rest[:-1], GROUP), rest[-1]
    sub, slab = place()
    group, pair = sub // 4, sub // 2 % 2
    even = sub % 2 == 0
    half = LANES // 2
    lane = lax.broadcasted_iota(jnp.int32, (8, LANES), 1)

    def left_part(value):
        return jnp.where(lane < half, value, 0.0)

    mine, other = left_part(first_two[...]), left_part(received[0][...])
    first = jnp.where(
        pair == 0, mine + pltpu.roll(other, half, 1), other + pltpu.roll(mine, half, 1)
    )
    first = jnp.where(even, first, jnp.zeros_like(first))

    slab_even = jnp.where(even, received[1][...], received[0][...])
    slab_odd = received[4][...] if len(received) > 4 else None
    below, above = neighbours(slab, sizes[1], slab_even, slab_odd)
    firsts = left_part(below) + pltpu.roll(left_part(above), half, 1)

    group_even = jnp.where(even, received[2][...], received[1][...])
    group_odd = jnp.where(even, received[3][...], received[2][...])
    left, right = neighbours(group, sizes[0] // 4, group_even, group_odd)
    width = GX // 4 * (GZ // 4)
    left = pltpu.roll(left, LANES - half - width, 1)
    right = pltpu.roll(right, LANES - half + width, 1)
    seconds = jnp.where(lane < width, left, jnp.where(lane < 2 * width, right, 0.0))

    table = table_four([first, firsts, seconds])
    mine = jnp.where(pair == 0, columns[...], pltpu.roll(columns[...], half, 1))
    total = None
    for k in range(7):
        near = twice(gather_four(table, mine[k : k + 1]))
        term = operator[16 * k : 16 * k + 16] * near
        total = term if total is None else total + term
    out[...] = sum_components(total)


def group_second(source, weights, first_two, own, other, out):
    sub, slab = place()
    residual = source[...] - (own[...] + other[...])
    second = first_two[...] + residual / weights[...]
    share = out.shape[1]
    out[...] = jnp.where(sub % 2 == 0, second[0:4, 0:share], second[0:4, share : 2 * share])


def swap_by_core(value, even_mate, odd_mate, spare=2):
    subs, slabs = lax.axis_size("sub"), lax.axis_size("slab")
    route = []
    for sub in range(subs):
        for slab in range(slabs):
            target = (even_mate if sub % 2 == 0 else odd_mate)(sub, slab)
            if not (0 <= target[0] < subs and 0 <= target[1] < slabs):
                target = (sub ^ spare, slab)
            route.append((sub * slabs + slab, target[0] * slabs + target[1]))
    return lax.ppermute(value, ("sub", "slab"), route)


def odd_mate_of(index):
    return ((index - 1) ^ 1) + 1


def group_exchange(whole, slab_values):
    def along_sub(odd, flip):
        def mate(sub, slab):
            block = odd_mate_of(sub // 4) if odd else sub // 4 ^ 1
            return block * 4 + (sub % 4 ^ flip), slab

        return mate

    def along_slab(odd, flip):
        return lambda sub, slab: (sub ^ flip, odd_mate_of(slab) if odd else slab ^ 1)

    def pair(sub, slab):
        return sub ^ 2, slab

    def idle(sub, slab):
        inside = 0 <= odd_mate_of(sub // 4) < lax.axis_size("sub") // 4
        return sub ^ (2 if inside else 1), slab

    first = slab_values[0]
    received = [
        swap_by_core(whole, pair, along_slab(False, 2)),
        swap_by_core(first, along_slab(False, 0), along_sub(False, 2)),
        swap_by_core(first, along_sub(False, 0), along_sub(True, 2)),
        swap_by_core(first, along_sub(True, 0), idle, spare=1),
    ]
    for value in slab_values[1:]:
        received.append(swap_by_core(value, along_slab(True, 0), along_slab(True, 2)))
    return received


def sub_pairing(value, group, odd):
    subs, slabs = lax.axis_size("sub"), lax.axis_size("slab")
    route = []
    for sub in range(subs):
        block = sub // group
        mate = ((block - 1) ^ 1) + 1 if odd else block ^ 1
        for slab in range(slabs):
            target = (mate * group + sub % group, slab)
            if not 0 <= mate < subs // group:
                target = (sub ^ group // 2, slab) if group > 1 else (sub, slab ^ 1)
            route.append((sub * slabs + slab, target[0] * slabs + target[1]))
    return lax.ppermute(value, ("sub", "slab"), route)


def slab_pairing(value, odd):
    subs, slabs = lax.axis_size("sub"), lax.axis_size("slab")
    route = []
    for sub in range(subs):
        for slab in range(slabs):
            mate = ((slab - 1) ^ 1) + 1 if odd else slab ^ 1
            target = (sub, mate) if 0 <= mate < slabs else (sub ^ 1, slab)
            route.append((sub * slabs + slab, target[0] * slabs + target[1]))
    return lax.ppermute(value, ("sub", "slab"), route)


def slab_pairings(values):
    return [slab_pairing(value, position == 1) for position, value in enumerate(values)]


def on_device(
    source,
    operator,
    prolong,
    columns,
    slots,
    aggregates,
    sends,
    prolong_one,
    columns_one,
    slots_one,
    aggregates_one,
    sends_one,
    columns_two,
    sends_two,
):
    sizes = (lax.axis_size("sub"), lax.axis_size("slab"))
    slab_moves = 1 if sizes[1] == 2 else 2
    rows = source.shape[1]
    rows_one = rows // 8
    pair_rows_one = 2 * rows_one
    count = 2 * GY * GZ
    kept = [
        source,
        sends,
        sends_one,
        columns,
        slots,
        aggregates,
        columns_one,
        slots_one,
        aggregates_one,
        columns_two,
        sends_two,
    ]
    raw = [operator, kept[0], prolong, kept[1], prolong_one, kept[2], *kept[3:]]
    handed = len(kept)
    out = call(
        functools.partial(fine_first, handed, slab_moves),
        [((1, value.shape[0]) if value.ndim == 1 else value.shape, value.dtype) for value in kept]
        + [operator.shape, (16, rows), (16, pair_rows_one)]
        + [(8, rows), (8, rows), (24, count), (24, count + LANES)]
        + [(24, count + LANES)] * slab_moves,
        *[pltpu.with_memory_space_constraint(value, pltpu.HBM) for value in raw],
        scratch=[
            pltpu.VMEM(prolong.shape, F32),
            pltpu.VMEM(prolong_one.shape, F32),
            pltpu.VMEM((24, rows), F32),
            pltpu.SemaphoreType.DMA((len(raw) - 1,)),
            pltpu.SemaphoreType.DMA((7,)),
        ],
        space=pltpu.HBM,
    )
    source, sends, sends_one, columns, slots, aggregates = out[:6]
    columns_one, slots_one, aggregates_one, columns_two, sends_two = out[6:11]
    operator_raw, prolong, prolong_one, weights, first, even, odd, *slabs = out[11:]
    even_old = sub_pairing(even, 1, False)
    odd_old = sub_pairing(odd, 1, True)
    slabs_old = slab_pairings(slabs)

    operator, own_near = call(
        fine_own,
        [(112, rows), (16 * OWN_SLOTS, rows)],
        operator_raw,
        prolong,
        columns,
        flops=10**9,
    )
    even, odd, *rest = call(
        functools.partial(fine_second, sizes),
        [(8, count + 2 * LANES), (8, count)]
        + [(8, count)] * slab_moves
        + [(8, rows)],
        source,
        operator,
        columns,
        sends,
        weights,
        first,
        *ordered([even_old, odd_old, *slabs_old], FINE_FIRST),
        scratch=[pltpu.VMEM((8, sends.shape[1]), F32)],
    )
    slabs, second = rest[:-1], rest[-1]
    forwarded = sub_pairing(even, 1, False)
    odd_in = sub_pairing(odd, 1, True)
    slabs_in = slab_pairings(slabs)

    (operator_own,) = call(
        functools.partial(fine_coarsen, sizes),
        [(112, rows_one)],
        operator,
        prolong,
        columns,
        slots,
        aggregates,
        own_near,
        second,
        even_old,
        odd_old,
        *slabs_old,
        scratch=[pltpu.VMEM((112, rows), F32)],
        flops=4 * 10**9,
    )
    (own,) = call(
        functools.partial(fine_restrict, sizes),
        [(120, rows_one)],
        source,
        operator,
        prolong,
        columns,
        aggregates,
        second,
        operator_own,
        *ordered([forwarded, odd_in, *slabs_in], FINE_SECOND),
        scratch=[pltpu.VMEM((8, rows), F32)],
    )
    other = sub_pairing(own, 1, False)

    faces = [(8, LANES)] * (1 + slab_moves)
    operator_one, source_one, weights_one, first_one, group_out, *slabs = call(
        pair_first,
        [(112, pair_rows_one)] + [(8, pair_rows_one)] * 3 + faces,
        own,
        other,
        sends_one,
    )
    even_in = sub_pairing(group_out, 2, False)
    odd_in = sub_pairing(group_out, 2, True)
    slabs_in = slab_pairings(slabs)

    second_one, group_out, *slabs = call(
        functools.partial(pair_second, sizes),
        [(8, pair_rows_one)] + faces,
        operator_one,
        source_one,
        weights_one,
        first_one,
        columns_one,
        sends_one,
        *ordered([even_in, odd_in, *slabs_in], PAIR_FIRST),
    )
    even_in = sub_pairing(group_out, 2, False)
    odd_in = sub_pairing(group_out, 2, True)
    slabs_in = slab_pairings(slabs)

    operator_two, weights_two, smoothed, smoothed_one = call(
        functools.partial(pair_coarsen, sizes),
        [(112, LANES), (8, LANES), (4, rows), (4, rows_one)],
        operator_one,
        prolong_one,
        columns_one,
        slots_one,
        aggregates_one,
        second,
        second_one,
        even_old,
        odd_old,
        forwarded,
        *slabs_old,
        scratch=[pltpu.VMEM((112, pair_rows_one), F32)],
        flops=10**9,
    )
    source_two, first_two, whole, *slabs = call(
        functools.partial(pair_restrict, sizes),
        [(8, LANES), (8, LANES)] + faces,
        operator_one,
        source_one,
        second_one,
        prolong_one,
        columns_one,
        aggregates_one,
        sends_two,
        weights_two,
        *ordered([even_in, odd_in, *slabs_in], PAIR_SECOND),
        scratch=[pltpu.VMEM((8, pair_rows_one), F32)],
    )
    received = group_exchange(whole, slabs)
    (applied,) = call(
        functools.partial(group_apply, sizes),
        [(8, LANES)],
        operator_two,
        first_two,
        columns_two,
        *ordered(received, GROUP),
    )
    applied_other = sub_pairing(applied, 1, False)
    (smoothed_two,) = call(
        group_second,
        [(4, rows_one // 8)],
        source_two,
        weights_two,
        first_two,
        applied,
        applied_other,
    )
    return (smoothed, smoothed_one, smoothed_two)


def solution(mesh):
    placed = (
        P(None, ("sub", "slab")),
        P(None, None, None, ("sub", "slab")),
        P(None, None, ("sub", "slab")),
        P(None, ("sub", "slab")),
        P(None, ("sub", "slab")),
        P(("sub", "slab")),
        P(("sub", "slab")),
        P(None, None, ("sub", "slab")),
        P(None, ("sub", "slab")),
        P(None, ("sub", "slab")),
        P(("sub", "slab")),
        P(("sub", "slab")),
        P(None, ("sub", "slab")),
        P(("sub", "slab")),
    )
    return jax.shard_map(
        on_device,
        mesh=mesh,
        in_specs=placed,
        out_specs=(P(None, ("sub", "slab")), P(None, ("sub", "slab")), P(None, ("sub", "slab"))),
        check_vma=False,
    )
```

```python
import functools

import jax
import jax.numpy as jnp
from jax import lax
from jax.experimental import pallas as pl
from jax.experimental.pallas import tpu as pltpu
from jax.sharding import PartitionSpec as P

GX = 8
GY = 8
GZ = 32
LANES = 128
OWN_SLOTS = 7
FINE_FIRST = (0, 1, 2)
FINE_SECOND = (0, 1, 2)
GROUP = (0, 3, 2, 1)


def ordered(values, order):
    return [values[at] for at in order] + list(values[len(order) :])


def restored(refs, order):
    return [refs[order.index(at)] for at in range(len(order))] + list(refs[len(order) :])
F32 = jnp.float32
BF16 = jnp.bfloat16


def split(value):
    high = value.astype(BF16)
    return high, (value - high.astype(F32)).astype(BF16)


def upper_half(shape):
    return lax.broadcasted_iota(jnp.int32, shape, 0) >= 4


def fold(value):
    return value + pltpu.roll(value, 4, 0)


def pair_rows(first, second):
    return jnp.where(upper_half(first.shape), second, first)


def twice(rows):
    return jnp.concatenate([rows, rows], axis=0)


def table_four(chunks):
    if len(chunks) % 2:
        chunks = chunks + [jnp.zeros_like(chunks[0])]
    rows = [pair_rows(chunks[j], chunks[j + 1]) for j in range(0, len(chunks), 2)]
    return jnp.concatenate(split(jnp.concatenate(rows, axis=0)), axis=1)


def table_sixteen(chunks):
    return jnp.concatenate(split(jnp.concatenate(chunks, axis=0)), axis=1)


def onehot(columns):
    low = (columns & (LANES - 1)).astype(jnp.int16)
    low = jnp.broadcast_to(low, (LANES, columns.shape[1]))
    here = lax.broadcasted_iota(jnp.int16, low.shape, 0) == low
    return twice(jnp.where(here, jnp.ones((), BF16), jnp.zeros((), BF16)))


def choose_four(picked, high):
    shape = (8, picked.shape[1])
    high = jnp.broadcast_to(high, shape) - upper_half(shape).astype(jnp.int32)
    total = jnp.zeros(shape, F32)
    for j in range(picked.shape[0] // 8):
        total = jnp.where(high == 2 * j, picked[8 * j : 8 * j + 8], total)
    return fold(total)


def choose_sixteen(picked, high):
    shape = (8, picked.shape[1])
    high = jnp.broadcast_to(high, shape)
    total = [jnp.zeros(shape, F32), jnp.zeros(shape, F32)]
    for j in range(picked.shape[0] // 16):
        here = high == j
        for half in range(2):
            at = 16 * j + 8 * half
            total[half] = jnp.where(here, picked[at : at + 8], total[half])
    return total


def matmul(left, right):
    return jnp.dot(left, right, preferred_element_type=F32)


def gather_four(table, columns):
    return choose_four(matmul(table, onehot(columns)), columns >> 7)


def gather_halves(table, columns, chunk):
    return choose_sixteen(matmul(table, onehot(columns)), (columns >> 7) - chunk)


def gather_sixteen(table, columns):
    return jnp.concatenate(gather_halves(table, columns, 0), axis=0)


def sum_components(value):
    first = value.astype(BF16)
    rest = value - first.astype(F32)
    second = rest.astype(BF16)
    third = (rest - second.astype(F32)).astype(BF16)
    row = lax.broadcasted_iota(jnp.int32, (8, 48), 0) & 3
    column = (lax.broadcasted_iota(jnp.int32, (8, 48), 1) >> 2) & 3
    ones = (row == column).astype(F32).astype(BF16)
    return matmul(ones, jnp.concatenate([first, second, third], axis=0))


def row_weights(operator_at):
    total = jnp.abs(operator_at(0))
    for k in range(1, 7):
        total = total + jnp.abs(operator_at(k))
    return 1.0 + sum_components(total)


def lift(prolong, residual):
    second = upper_half(residual.shape).astype(jnp.int32)
    low = jnp.take_along_axis(residual, second, axis=0)
    high = jnp.take_along_axis(residual, second + 2, axis=0)
    return fold(prolong[:8] * low + prolong[8:] * high)


def expand(rows):
    shape = (8, rows.shape[1])
    second = upper_half(shape).astype(jnp.int32)
    return [
        [
            jnp.take_along_axis(
                rows[8 * (a // 2) : 8 * (a // 2) + 8], second + (4 * (a % 2) + 2 * h), axis=0
            )
            for h in (0, 1)
        ]
        for a in range(4)
    ]


def triple_product(wide_prolong, operator, near):
    wide = expand(operator)
    out = [None, None]
    for a in range(4):
        inner = fold(wide[a][0] * near[0] + wide[a][1] * near[1])
        for half in range(2):
            term = wide_prolong[a][half] * inner
            out[half] = term if out[half] is None else out[half] + term
    return out


def onehot_rows(targets, count):
    shape = (count, targets.shape[1])
    here = lax.broadcasted_iota(jnp.int32, shape, 0) == jnp.broadcast_to(targets, shape)
    return here.astype(F32).astype(BF16)


def scatter(values, targets, count):
    return add_up(values, onehot_rows(targets, count))


def add_up(values, hot):
    high, low = split(values)
    both = lax.dot_general(
        jnp.concatenate([high, low], axis=0),
        hot,
        (((1,), (1,)), ((), ())),
        preferred_element_type=F32,
    )
    rows = values.shape[0]
    return both[:rows] + both[rows:]


def chunks_of(value):
    return [value[:, at : at + LANES] for at in range(0, value.shape[1], LANES)]


def place():
    sub, slab = lax.axis_index("sub"), lax.axis_index("slab")
    return sub, slab


def neighbours(index, count, even, odd):
    is_even = index % 2 == 0
    if odd is None:
        odd = jnp.zeros_like(even)
    below = jnp.where(is_even, odd, even)
    above = jnp.where(is_even, even, odd)
    below = jnp.where(index > 0, below, jnp.zeros_like(below))
    above = jnp.where(index < count - 1, above, jnp.zeros_like(above))
    return below, above


def swap_halves(below, above, half):
    lane = lax.broadcasted_iota(jnp.int32, below.shape, 1)
    return pltpu.roll(jnp.where(lane < half, above, below), half, 1)


def call(body, outs, *args, scratch=(), flops=0, space=pltpu.VMEM):
    outs = [(out, F32) if isinstance(out[0], int) else out for out in outs]
    cost = pl.CostEstimate(flops=flops, bytes_accessed=0, transcendentals=0) if flops else None
    return pl.pallas_call(
        body,
        out_shape=[jax.ShapeDtypeStruct(shape, dtype) for shape, dtype in outs],
        in_specs=[pl.BlockSpec(memory_space=space)] * len(args),
        out_specs=[pl.BlockSpec(memory_space=pltpu.VMEM)] * len(outs),
        scratch_shapes=list(scratch),
        cost_estimate=cost,
        compiler_params=pltpu.CompilerParams(vmem_limit_bytes=32 * 1024 * 1024),
    )(*args)


def tiles(count, tile, body):
    def step(index, carry):
        body(pl.ds(pl.multiple_of(index * tile, tile), tile))
        return carry

    lax.fori_loop(0, count // tile, step, 0, unroll=True)


def fine_first(handed, slab_moves, *refs):
    count = handed + 3
    raw, refs = refs[:count], refs[count:]
    kept, refs = refs[:handed], refs[handed:]
    operator_raw, prolong, prolong_one, w_ref, first_ref, parity_out, cross_out = refs[:7]
    slab_outs, refs = refs[7 : 7 + slab_moves], refs[7 + slab_moves :]
    prolong_raw, prolong_one_raw, picks, wide_picks, semaphores, slot_semaphores = refs
    source, sends, sends_one = kept[0], kept[1], kept[2]
    targets = [prolong_raw, sends, prolong_one_raw, sends_one, source, *kept[3:]]
    sources = [raw[2], raw[3], raw[4], raw[5], raw[1], *raw[6:]]
    copies = [
        pltpu.make_async_copy(
            value, target if value.ndim > 1 else target.at[0], semaphores.at[at]
        )
        for at, (value, target) in enumerate(zip(sources, targets))
    ]
    slot_copies = [
        pltpu.make_async_copy(raw[0].at[k], operator_raw.at[k], slot_semaphores.at[k])
        for k in range(7)
    ]
    for copy in copies[:5] + slot_copies + copies[5:]:
        copy.start()

    copies[0].wait()
    copies[1].wait()
    for half in range(2):
        at = slice(8 * half, 8 * half + 8)
        prolong[at] = jnp.concatenate([prolong_raw[2 * half], prolong_raw[2 * half + 1]], axis=0)
    wide_table = table_sixteen(chunks_of(prolong[...]))

    def pick_wide(at):
        wide_picks[:, at] = gather_sixteen(wide_table, sends[:, at])

    tiles(sends.shape[1], 512, pick_wide)
    copies[2].wait()
    copies[3].wait()
    for half in range(2):
        at = slice(8 * half, 8 * half + 8)
        prolong_one[at] = jnp.concatenate(
            [prolong_one_raw[2 * half], prolong_one_raw[2 * half + 1]], axis=0
        )
    coarse = gather_sixteen(table_sixteen(chunks_of(prolong_one[...])), sends_one[...])
    sub, slab = place()
    even = sub % 2 == 0
    count = sends.shape[1] // 4
    low_first, high_first = wide_picks[:, 0:count], wide_picks[:, count : 2 * count]
    low_second, high_second = wide_picks[:, 2 * count : 3 * count], wide_picks[:, 3 * count :]
    parity_out[:, 0:count] = jnp.where(even, high_second, low_second)
    cross_out[:, 0:count] = jnp.where(even, low_second, high_second)
    cross_out[:, count + LANES :] = coarse[:, 2 * LANES :]
    for position, out in enumerate(slab_outs):
        up = slab % 2 == position
        out[:, 0:count] = jnp.where(up, high_first, low_first)
        out[:, count + LANES :] = jnp.where(up, coarse[:, LANES : 2 * LANES], coarse[:, 0:LANES])

    sums = [None] * 4
    for k in range(7):
        slot_copies[k].wait()
        for a in range(4):
            value = jnp.abs(operator_raw[k, a])
            sums[a] = value if sums[a] is None else sums[a] + value
    weights = 1.0 + sum_components(jnp.concatenate(sums, axis=0))
    copies[4].wait()
    first = twice(source[...]) / weights
    w_ref[...] = weights
    first_ref[...] = first
    table = table_four(chunks_of(first))
    at = slice(count, count + LANES)
    faces = fine_faces(table, sends, picks)
    parity, cross, slabs = chosen_faces(faces, sub, slab, len(slab_outs))
    parity_out[:, at] = parity
    cross_out[:, at] = cross
    for out, value in zip(slab_outs, slabs):
        out[:, at] = value
    for copy in copies[5:]:
        copy.wait()


def fine_faces(table, sends, picks):
    def pick(at):
        picks[:, at] = gather_four(table, sends[:, at])

    tiles(sends.shape[1], 1024, pick)
    rows = [picks[0:4, at : at + LANES] for at in range(0, sends.shape[1], LANES)]
    each = len(rows) // 4
    return [jnp.concatenate(rows[each * at : each * at + each], axis=0) for at in range(4)]


def chosen_faces(faces, sub, slab, slab_count):
    low_first, high_first, low_second, high_second = faces
    even = sub % 2 == 0
    parity = jnp.where(even, high_second, low_second)
    cross = jnp.where(even, low_second, high_second)
    slabs = [jnp.where(slab % 2 == at, high_first, low_first) for at in range(slab_count)]
    return parity, cross, slabs


def fine_own(operator_raw, prolong, columns, operator, own_near):
    table = table_sixteen(chunks_of(prolong[...]))

    def step(at):
        for k in range(own_near.shape[0] // 16):
            low, high = gather_halves(table, columns[k : k + 1, at], 0)
            own_near[16 * k : 16 * k + 8, at] = low
            own_near[16 * k + 8 : 16 * k + 16, at] = high

    tiles(columns.shape[1], 512, step)
    for k in range(7):
        for half in range(2):
            row = 16 * k + 8 * half
            operator[row : row + 8] = jnp.concatenate(
                [operator_raw[k, 2 * half], operator_raw[k, 2 * half + 1]], axis=0
            )


def fine_ghosts(at, sizes, parity_in, cross_in, slab_ins):
    sub, slab = place()
    slab_values = [ref[:, at] for ref in slab_ins] + [None]
    below, above = neighbours(slab, sizes[1], slab_values[0], slab_values[1])
    left, right = neighbours(sub, sizes[0], parity_in[:, at], cross_in[:, at])
    return [below, above, left, right]


def four_chunks(faces):
    return [twice(face[at : at + 4]) for face in faces for at in range(0, face.shape[0], 4)]


def sixteen_chunks(faces):
    return [chunk for face in faces for chunk in chunks_of(face)]


def apply_tile(table, operator, columns, at):
    total = None
    for k in range(7):
        near = twice(gather_four(table, columns[k : k + 1, at]))
        term = operator[16 * k : 16 * k + 16, at] * near
        total = term if total is None else total + term
    return sum_components(total)


def fine_second(
    sizes, source, operator, columns, sends, w_ref, first_ref, *rest
):
    slab_count = (len(rest) - 6) // 2
    taken, rest = restored(rest[: slab_count + 2], FINE_FIRST), rest[slab_count + 2 :]
    parity_in, cross_in, *slab_ins = taken
    parity_out, cross_out = rest[0], rest[1]
    slab_outs, second_ref, picks = rest[2:-2], rest[-2], rest[-1]
    count = sends.shape[1] // 4
    ghosts = fine_ghosts(
        slice(count, count + LANES), sizes, parity_in, cross_in, slab_ins
    )
    table = table_four(chunks_of(first_ref[...]) + four_chunks(ghosts))

    def step(at):
        residual = twice(source[:, at]) - apply_tile(table, operator, columns, at)
        second_ref[:, at] = first_ref[:, at] + residual / w_ref[:, at]

    tiles(source.shape[1], source.shape[1], step)
    faces = fine_faces(table_four(chunks_of(second_ref[...])), sends, picks)
    sub, slab = place()
    parity, cross, slabs = chosen_faces(faces, sub, slab, len(slab_outs))
    parity_out[:, 0:LANES] = parity
    parity_out[:, LANES:] = cross_in[:, count + LANES :]
    cross_out[...] = cross
    for out, value in zip(slab_outs, slabs):
        out[...] = value


def coarsen(tables, operator, prolong, columns, slots, aggregates, sums, count, own_near=None):
    tile = 256
    whole = jnp.concatenate(tables, axis=0)
    known = 0 if own_near is None else own_near.shape[0] // 16

    def step(at):
        wide_prolong = expand(prolong[:, at])
        totals = [[jnp.zeros((8, tile), F32) for _ in range(2)] for _ in range(7)]
        for k in range(7):
            column = columns[k : k + 1, at]
            if k < known:
                near = gather_halves(tables[1], column, tables[0].shape[0] // 16)
                near = [
                    near[half] + own_near[16 * k + 8 * half : 16 * k + 8 * half + 8, at]
                    for half in range(2)
                ]
            else:
                near = gather_halves(whole, column, 0)
            blocks = triple_product(wide_prolong, operator[16 * k : 16 * k + 16, at], near)
            slot = jnp.broadcast_to(slots[k : k + 1, at], (8, tile))
            for s in range(7):
                here = slot == s
                for half in range(2):
                    totals[s][half] = totals[s][half] + jnp.where(here, blocks[half], 0.0)
        for s in range(7):
            for half in range(2):
                row = 16 * s + 8 * half
                sums[row : row + 8, at] = totals[s][half]

    tiles(columns.shape[1], tile, step)
    return scatter(sums[...], aggregates[...], count)


def fine_coarsen(
    sizes,
    operator,
    prolong,
    columns,
    slots,
    aggregates,
    own_near,
    second_ref,
    parity_old,
    cross_old,
    *rest,
):
    slab_old, (out, sums) = rest[:-2], rest[-2:]
    count = parity_old.shape[1] - LANES
    ghosts = fine_ghosts(slice(0, count), sizes, parity_old, cross_old, slab_old)
    tables = [table_sixteen(chunks_of(prolong[...])), table_sixteen(sixteen_chunks(ghosts))]
    out[...] = coarsen(
        tables, operator, prolong, columns, slots, aggregates, sums, out.shape[1], own_near
    )


def fine_restrict(
    sizes,
    source,
    operator,
    prolong,
    columns,
    aggregates,
    second_ref,
    operator_own,
    *rest,
):
    parity_in, cross_in, *slab_ins = restored(rest[:-2], FINE_SECOND)
    out, lifted = rest[-2:]
    ghosts = fine_ghosts(slice(0, LANES), sizes, parity_in, cross_in, slab_ins)
    table = table_four(chunks_of(second_ref[...]) + four_chunks(ghosts))

    def step(at):
        residual = twice(source[:, at]) - apply_tile(table, operator, columns, at)
        lifted[:, at] = lift(prolong[:, at], residual)

    tiles(source.shape[1], source.shape[1], step)
    out[0:112] = operator_own[...]
    out[112:120] = scatter(lifted[...], aggregates[...], out.shape[1])


def pair_faces(picks, sub, slab, outs):
    for position, out in enumerate(outs):
        face = jnp.where(
            slab % 2 == position, picks[:, LANES : 2 * LANES], picks[:, 0:LANES]
        )
        out[...] = jnp.where(sub % 2 == 0, face, picks[:, 2 * LANES :])


def pair_first(own, other, sends, operator, source, weights, first, *outs):
    sub, slab = place()
    even = sub % 2 == 0
    half = own.shape[1]
    lower = jnp.where(even, own[...], other[...])
    upper = jnp.where(even, other[...], own[...])
    operator[:, 0:half] = lower[0:112]
    operator[:, half:] = upper[0:112]
    source[:, 0:half] = lower[112:120]
    source[:, half:] = upper[112:120]
    weights[...] = row_weights(lambda k: operator[16 * k : 16 * k + 16])
    first[...] = source[...] / weights[...]
    picks = gather_four(table_four(chunks_of(first[...])), sends[...])
    pair_faces(picks, sub, slab, outs)


def pair_ghosts(sizes, mine, other):
    sub, slab = place()
    even = sub % 2 == 0
    mine, other = [mine[0:8], mine[8:16]], [other[0:8], other[8:16]]
    along_slab = [jnp.where(even, mine[at], other[at]) for at in range(2)]
    along_sub = [jnp.where(even, other[at], mine[at]) for at in range(2)]
    below, above = neighbours(
        slab, sizes[1], along_slab[0], along_slab[1] if sizes[1] > 2 else None
    )
    left, right = neighbours(sub // 2, sizes[0] // 2, along_sub[0], along_sub[1])
    return [below, above, swap_halves(left, right, LANES // 2)]


def pair_second(
    sizes, operator, source, weights, first, columns, sends, mine, other, second_ref, *outs
):
    table = table_four(chunks_of(first[...]) + pair_ghosts(sizes, mine, other))

    def step(at):
        residual = source[:, at] - apply_tile(table, operator, columns, at)
        second_ref[:, at] = first[:, at] + residual / weights[:, at]

    tiles(source.shape[1], 512, step)
    sub, slab = place()
    picks = gather_four(table_four(chunks_of(second_ref[...])), sends[...])
    pair_faces(picks, sub, slab, outs)


def pair_coarsen(
    sizes,
    operator,
    prolong,
    columns,
    slots,
    aggregates,
    sends,
    second_fine,
    second_ref,
    parity_old,
    cross_old,
    forwarded,
    *rest,
):
    slab_old, rest = rest[:-7], rest[-7:]
    operator_two, weights_two, face_weights, hot_out, smoothed, smoothed_one, sums = rest
    sub, slab = place()
    even = sub % 2 == 0
    half = smoothed_one.shape[1]
    smoothed[...] = second_fine[0:4]
    smoothed_one[...] = jnp.where(even, second_ref[0:4, 0:half], second_ref[0:4, half:])
    after = parity_old.shape[1]
    values = [ref[:, after:] for ref in slab_old] + [None]
    below, above = neighbours(slab, sizes[1], values[0], values[1])
    mine = cross_old[:, after:]
    partners = forwarded[:, LANES:]
    group = sub // 2
    left = jnp.where(even, mine, partners)
    right = jnp.where(even, partners, mine)
    left = jnp.where(group > 0, left, jnp.zeros_like(left))
    right = jnp.where(group < sizes[0] // 2 - 1, right, jnp.zeros_like(right))
    ghosts = [below, above, swap_halves(left, right, LANES // 2)]
    tables = [table_sixteen(chunks_of(prolong[...])), table_sixteen(ghosts)]
    operator_two[...] = coarsen(
        tables, operator, prolong, columns, slots, aggregates, sums, LANES
    )
    weights = row_weights(lambda k: operator_two[16 * k : 16 * k + 16])
    weights_two[...] = weights
    filler = jnp.zeros((1, -sends.shape[1] % LANES), jnp.int32)
    rows = jnp.concatenate([sends[...], filler], axis=1) - group % 2 * (LANES // 2)
    face_weights[...] = gather_four(table_four([weights]), rows & (LANES - 1))
    hot = onehot_rows(aggregates[...], LANES)
    hot_out[0:LANES] = hot
    hot_out[LANES:] = lax.dot_general(
        onehot(rows)[0:LANES], hot, (((0,), (0,)), ((), ())), preferred_element_type=F32
    ).astype(BF16)


def pair_restrict(
    sizes,
    operator,
    source,
    second_ref,
    prolong,
    columns,
    weights_two,
    face_weights,
    hot,
    *rest,
):
    mine, other, *rest = rest
    source_two, first_two, whole_out = rest[:3]
    slab_outs, lifted = rest[3:-1], rest[-1]
    sub, slab = place()
    table = table_four(chunks_of(second_ref[...]) + pair_ghosts(sizes, mine, other))

    def step(at):
        residual = source[:, at] - apply_tile(table, operator, columns, at)
        lifted[:, at] = lift(prolong[:, at], residual)

    tiles(source.shape[1], 512, step)
    totals = add_up(lifted[...], hot[...])
    total = totals[:, 0:LANES]
    source_two[...] = total
    first = total / weights_two[...]
    first_two[...] = first
    half = LANES // 2
    lane = lax.broadcasted_iota(jnp.int32, first.shape, 1)
    picks = totals[:, LANES:] / face_weights[...]
    faces = picks[:, 0:LANES]
    seconds = pltpu.roll(picks[:, LANES:], half, 1)

    def sent(value):
        return jnp.where(lane < half, value, seconds)

    slab_even = slab % 2 == 0
    for position, out in enumerate(slab_outs):
        up = slab_even if position == 0 else jnp.logical_not(slab_even)
        out[...] = sent(jnp.where(up, pltpu.roll(faces, half, 1), faces))
    whole_out[...] = jnp.where(sub % 2 == 0, sent(first), slab_outs[0][...])


def group_apply(sizes, operator, first_two, columns, *rest):
    received, out = restored(rest[:-1], GROUP), rest[-1]
    sub, slab = place()
    group, pair = sub // 4, sub // 2 % 2
    even = sub % 2 == 0
    half = LANES // 2
    lane = lax.broadcasted_iota(jnp.int32, (8, LANES), 1)

    def left_part(value):
        return jnp.where(lane < half, value, 0.0)

    mine, other = left_part(first_two[...]), left_part(received[0][...])
    first = jnp.where(
        pair == 0, mine + pltpu.roll(other, half, 1), other + pltpu.roll(mine, half, 1)
    )
    first = jnp.where(even, first, jnp.zeros_like(first))

    slab_even = jnp.where(even, received[1][...], received[0][...])
    slab_odd = received[4][...] if len(received) > 4 else None
    below, above = neighbours(slab, sizes[1], slab_even, slab_odd)
    firsts = left_part(below) + pltpu.roll(left_part(above), half, 1)

    group_even = jnp.where(even, received[2][...], received[1][...])
    group_odd = jnp.where(even, received[3][...], received[2][...])
    left, right = neighbours(group, sizes[0] // 4, group_even, group_odd)
    width = GX // 4 * (GZ // 4)
    left = pltpu.roll(left, LANES - half - width, 1)
    right = pltpu.roll(right, LANES - half + width, 1)
    seconds = jnp.where(lane < width, left, jnp.where(lane < 2 * width, right, 0.0))

    table = table_four([first, firsts, seconds])
    mine = jnp.where(pair == 0, columns[...], pltpu.roll(columns[...], half, 1))
    total = None
    for k in range(7):
        near = twice(gather_four(table, mine[k : k + 1]))
        term = operator[16 * k : 16 * k + 16] * near
        total = term if total is None else total + term
    out[...] = sum_components(total)


def group_second(source, weights, first_two, own, other, out):
    sub, slab = place()
    residual = source[...] - (own[...] + other[...])
    second = first_two[...] + residual / weights[...]
    share = out.shape[1]
    out[...] = jnp.where(sub % 2 == 0, second[0:4, 0:share], second[0:4, share : 2 * share])


def other_core(sub, slab):
    return sub ^ 1, slab


def swap_by_core(value, even_mate, odd_mate, even_spare=None, odd_spare=None):
    subs, slabs = lax.axis_size("sub"), lax.axis_size("slab")
    route = []
    for sub in range(subs):
        for slab in range(slabs):
            even = sub % 2 == 0
            target = (even_mate if even else odd_mate)(sub, slab)
            if not (0 <= target[0] < subs and 0 <= target[1] < slabs):
                spare = even_spare if even else odd_spare
                target = (sub ^ 2, slab) if spare is None else spare(sub, slab)
            route.append((sub * slabs + slab, target[0] * slabs + target[1]))
    return lax.ppermute(value, ("sub", "slab"), route)


def odd_mate_of(index):
    return ((index - 1) ^ 1) + 1


def along_sub(group, odd, flip):
    def mate(sub, slab):
        block = odd_mate_of(sub // group) if odd else sub // group ^ 1
        return block * group + (sub % group ^ flip), slab

    return mate


def along_slab(odd, flip):
    return lambda sub, slab: (sub ^ flip, odd_mate_of(slab) if odd else slab ^ 1)


def pair_exchange(first, second, beside=lambda: ()):
    def idle(sub, slab):
        inside = 0 <= odd_mate_of(sub // 2) < lax.axis_size("sub") // 2
        return (sub, slab ^ 1) if inside else (sub ^ 1, slab)

    def beside_slab(sub, slab):
        return sub, slab ^ 1

    last = along_sub(2, True, 0)
    received = [swap_by_core(first, along_slab(False, 0), along_sub(2, False, 0))]
    if lax.axis_size("slab") > 2:
        received.append(swap_by_core(second, along_slab(True, 0), last, None, beside_slab))
    else:
        received.append(swap_by_core(second, idle, last, None, other_core))
    mine = jnp.concatenate(received, axis=0)
    mine, results = lax.optimization_barrier((mine, beside()))
    return mine, sub_pairing(mine, 1, False), results


def group_exchange(whole, slab_values):
    def pair(sub, slab):
        return sub ^ 2, slab

    def idle(sub, slab):
        inside = 0 <= odd_mate_of(sub // 4) < lax.axis_size("sub") // 4
        return sub ^ (2 if inside else 1), slab

    first = slab_values[0]
    received = [
        swap_by_core(whole, pair, along_slab(False, 2)),
        swap_by_core(first, along_slab(False, 0), along_sub(4, False, 2)),
        swap_by_core(first, along_sub(4, False, 0), along_sub(4, True, 2)),
        swap_by_core(first, along_sub(4, True, 0), idle, other_core, other_core),
    ]
    for value in slab_values[1:]:
        received.append(swap_by_core(value, along_slab(True, 0), along_slab(True, 2)))
    return received


def sub_pairing(value, group, odd):
    subs, slabs = lax.axis_size("sub"), lax.axis_size("slab")
    route = []
    for sub in range(subs):
        block = sub // group
        mate = ((block - 1) ^ 1) + 1 if odd else block ^ 1
        for slab in range(slabs):
            target = (mate * group + sub % group, slab)
            if not 0 <= mate < subs // group:
                target = (sub ^ group // 2, slab) if group > 1 else (sub, slab ^ 1)
            route.append((sub * slabs + slab, target[0] * slabs + target[1]))
    return lax.ppermute(value, ("sub", "slab"), route)


def slab_pairing(value, odd):
    subs, slabs = lax.axis_size("sub"), lax.axis_size("slab")
    route = []
    for sub in range(subs):
        for slab in range(slabs):
            mate = ((slab - 1) ^ 1) + 1 if odd else slab ^ 1
            target = (sub, mate) if 0 <= mate < slabs else (sub ^ 1, slab)
            route.append((sub * slabs + slab, target[0] * slabs + target[1]))
    return lax.ppermute(value, ("sub", "slab"), route)


def slab_pairings(values):
    return [slab_pairing(value, position == 1) for position, value in enumerate(values)]


def on_device(
    source,
    operator,
    prolong,
    columns,
    slots,
    aggregates,
    sends,
    prolong_one,
    columns_one,
    slots_one,
    aggregates_one,
    sends_one,
    columns_two,
    sends_two,
):
    sizes = (lax.axis_size("sub"), lax.axis_size("slab"))
    slab_moves = 1 if sizes[1] == 2 else 2
    rows = source.shape[1]
    rows_one = rows // 8
    pair_rows_one = 2 * rows_one
    count = 2 * GY * GZ
    kept = [
        source,
        sends,
        sends_one,
        columns,
        slots,
        aggregates,
        columns_one,
        slots_one,
        aggregates_one,
        columns_two,
        sends_two,
    ]
    raw = [operator, kept[0], prolong, kept[1], prolong_one, kept[2], *kept[3:]]
    handed = len(kept)
    out = call(
        functools.partial(fine_first, handed, slab_moves),
        [((1, value.shape[0]) if value.ndim == 1 else value.shape, value.dtype) for value in kept]
        + [operator.shape, (16, rows), (16, pair_rows_one)]
        + [(8, rows), (8, rows), (16, count + LANES), (16, count + 2 * LANES)]
        + [(16, count + 2 * LANES)] * slab_moves,
        *[pltpu.with_memory_space_constraint(value, pltpu.HBM) for value in raw],
        scratch=[
            pltpu.VMEM(prolong.shape, F32),
            pltpu.VMEM(prolong_one.shape, F32),
            pltpu.VMEM((8, rows), F32),
            pltpu.VMEM((16, rows), F32),
            pltpu.SemaphoreType.DMA((len(raw) - 1,)),
            pltpu.SemaphoreType.DMA((7,)),
        ],
        space=pltpu.HBM,
    )
    source, sends, sends_one, columns, slots, aggregates = out[:6]
    columns_one, slots_one, aggregates_one, columns_two, sends_two = out[6:11]
    operator_raw, prolong, prolong_one, weights, first, even, odd, *slabs = out[11:]
    even_old = sub_pairing(even, 1, False)
    odd_old = sub_pairing(odd, 1, True)
    slabs_old = slab_pairings(slabs)

    operator, own_near = call(
        fine_own,
        [(112, rows), (16 * OWN_SLOTS, rows)],
        operator_raw,
        prolong,
        columns,
        flops=10**9,
    )
    even, odd, *rest = call(
        functools.partial(fine_second, sizes),
        [(16, 2 * LANES), (16, LANES)]
        + [(16, LANES)] * slab_moves
        + [(8, rows)],
        source,
        operator,
        columns,
        sends,
        weights,
        first,
        *ordered([even_old, odd_old, *slabs_old], FINE_FIRST),
        scratch=[pltpu.VMEM((8, sends.shape[1]), F32)],
    )
    slabs, second = rest[:-1], rest[-1]
    forwarded = sub_pairing(even, 1, False)
    odd_in = sub_pairing(odd, 1, True)
    slabs_in = slab_pairings(slabs)

    (operator_own,) = call(
        functools.partial(fine_coarsen, sizes),
        [(112, rows_one)],
        operator,
        prolong,
        columns,
        slots,
        aggregates,
        own_near,
        second,
        even_old,
        odd_old,
        *slabs_old,
        scratch=[pltpu.VMEM((112, rows), F32)],
        flops=4 * 10**9,
    )
    (own,) = call(
        functools.partial(fine_restrict, sizes),
        [(120, rows_one)],
        source,
        operator,
        prolong,
        columns,
        aggregates,
        second,
        operator_own,
        *ordered([forwarded, odd_in, *slabs_in], FINE_SECOND),
        scratch=[pltpu.VMEM((8, rows), F32)],
    )
    other = sub_pairing(own, 1, False)

    faces = [(8, LANES)] * (1 + slab_moves)
    pair_sent = [(8, LANES)] * 2
    operator_one, source_one, weights_one, first_one, *sent = call(
        pair_first,
        [(112, pair_rows_one)] + [(8, pair_rows_one)] * 3 + pair_sent,
        own,
        other,
        sends_one,
    )
    mine, other, _ = pair_exchange(*sent)

    second_one, *sent = call(
        functools.partial(pair_second, sizes),
        [(8, pair_rows_one)] + pair_sent,
        operator_one,
        source_one,
        weights_one,
        first_one,
        columns_one,
        sends_one,
        mine,
        other,
    )
    def coarse_operator():
        return call(
            functools.partial(pair_coarsen, sizes),
            [(112, LANES), (8, LANES), (8, 2 * LANES), ((3 * LANES, pair_rows_one), BF16)]
            + [(4, rows), (4, rows_one)],
            operator_one,
            prolong_one,
            columns_one,
            slots_one,
            aggregates_one,
            sends_two,
            second,
            second_one,
            even_old,
            odd_old,
            forwarded,
            *slabs_old,
            scratch=[pltpu.VMEM((112, pair_rows_one), F32)],
            flops=10**9,
        )

    mine, other, outs = pair_exchange(*sent, beside=coarse_operator)
    operator_two, weights_two, face_weights, hot, smoothed, smoothed_one = outs

    source_two, first_two, whole, *slabs = call(
        functools.partial(pair_restrict, sizes),
        [(8, LANES), (8, LANES)] + faces,
        operator_one,
        source_one,
        second_one,
        prolong_one,
        columns_one,
        weights_two,
        face_weights,
        hot,
        mine,
        other,
        scratch=[pltpu.VMEM((8, pair_rows_one), F32)],
    )
    received = group_exchange(whole, slabs)
    (applied,) = call(
        functools.partial(group_apply, sizes),
        [(8, LANES)],
        operator_two,
        first_two,
        columns_two,
        *ordered(received, GROUP),
    )
    applied_other = sub_pairing(applied, 1, False)
    (smoothed_two,) = call(
        group_second,
        [(4, rows_one // 8)],
        source_two,
        weights_two,
        first_two,
        applied,
        applied_other,
    )
    return (smoothed, smoothed_one, smoothed_two)


def solution(mesh):
    placed = (
        P(None, ("sub", "slab")),
        P(None, None, None, ("sub", "slab")),
        P(None, None, ("sub", "slab")),
        P(None, ("sub", "slab")),
        P(None, ("sub", "slab")),
        P(("sub", "slab")),
        P(("sub", "slab")),
        P(None, None, ("sub", "slab")),
        P(None, ("sub", "slab")),
        P(None, ("sub", "slab")),
        P(("sub", "slab")),
        P(("sub", "slab")),
        P(None, ("sub", "slab")),
        P(("sub", "slab")),
    )
    return jax.shard_map(
        on_device,
        mesh=mesh,
        in_specs=placed,
        out_specs=(P(None, ("sub", "slab")), P(None, ("sub", "slab")), P(None, ("sub", "slab"))),
        check_vma=False,
    )
```

```python
import functools

import jax
import jax.numpy as jnp
from jax import lax
from jax.experimental import pallas as pl
from jax.experimental.pallas import tpu as pltpu
from jax.sharding import PartitionSpec as P

GX = 8
GY = 8
GZ = 32
LANES = 128
OWN_SLOTS = 7
FINE_FIRST = (0, 1, 2)
FINE_SECOND = (0, 1, 2)
GROUP = (0, 3, 2, 1)


def ordered(values, order):
    return [values[at] for at in order] + list(values[len(order) :])


def restored(refs, order):
    return [refs[order.index(at)] for at in range(len(order))] + list(refs[len(order) :])
F32 = jnp.float32
BF16 = jnp.bfloat16


def split(value):
    high = value.astype(BF16)
    return high, (value - high.astype(F32)).astype(BF16)


def upper_half(shape):
    return lax.broadcasted_iota(jnp.int32, shape, 0) >= 4


def fold(value):
    return value + pltpu.roll(value, 4, 0)


def pair_rows(first, second):
    return jnp.where(upper_half(first.shape), second, first)


def twice(rows):
    return jnp.concatenate([rows, rows], axis=0)


def table_four(chunks):
    if len(chunks) % 2:
        chunks = chunks + [jnp.zeros_like(chunks[0])]
    rows = [pair_rows(chunks[j], chunks[j + 1]) for j in range(0, len(chunks), 2)]
    return jnp.concatenate(split(jnp.concatenate(rows, axis=0)), axis=1)


def table_sixteen(chunks):
    return jnp.concatenate(split(jnp.concatenate(chunks, axis=0)), axis=1)


def onehot(columns):
    low = (columns & (LANES - 1)).astype(jnp.int16)
    low = jnp.broadcast_to(low, (LANES, columns.shape[1]))
    here = lax.broadcasted_iota(jnp.int16, low.shape, 0) == low
    return twice(jnp.where(here, jnp.ones((), BF16), jnp.zeros((), BF16)))


def choose_four(picked, high):
    shape = (8, picked.shape[1])
    high = jnp.broadcast_to(high, shape) - upper_half(shape).astype(jnp.int32)
    total = jnp.zeros(shape, F32)
    for j in range(picked.shape[0] // 8):
        total = jnp.where(high == 2 * j, picked[8 * j : 8 * j + 8], total)
    return fold(total)


def choose_sixteen(picked, high, total=None):
    shape = (8, picked.shape[1])
    high = jnp.broadcast_to(high, shape)
    total = [jnp.zeros(shape, F32)] * 2 if total is None else list(total)
    for j in range(picked.shape[0] // 16):
        here = high == j
        for half in range(2):
            at = 16 * j + 8 * half
            total[half] = jnp.where(here, picked[at : at + 8], total[half])
    return total


def matmul(left, right):
    return jnp.dot(left, right, preferred_element_type=F32)


def gather_four(table, columns):
    return choose_four(matmul(table, onehot(columns)), columns >> 7)


def gather_halves(table, columns, chunk, outside=None):
    return choose_sixteen(matmul(table, onehot(columns)), (columns >> 7) - chunk, outside)


def gather_sixteen(table, columns):
    return jnp.concatenate(gather_halves(table, columns, 0), axis=0)


def sum_components(value):
    first = value.astype(BF16)
    rest = value - first.astype(F32)
    second = rest.astype(BF16)
    third = (rest - second.astype(F32)).astype(BF16)
    row = lax.broadcasted_iota(jnp.int32, (8, 48), 0) & 3
    column = (lax.broadcasted_iota(jnp.int32, (8, 48), 1) >> 2) & 3
    ones = (row == column).astype(F32).astype(BF16)
    return matmul(ones, jnp.concatenate([first, second, third], axis=0))


def row_weights(operator_at):
    total = jnp.abs(operator_at(0))
    for k in range(1, 7):
        total = total + jnp.abs(operator_at(k))
    return 1.0 + sum_components(total)


def lift(prolong, residual):
    second = upper_half(residual.shape).astype(jnp.int32)
    low = jnp.take_along_axis(residual, second, axis=0)
    high = jnp.take_along_axis(residual, second + 2, axis=0)
    return fold(prolong[:8] * low + prolong[8:] * high)


def expand(rows):
    shape = (8, rows.shape[1])
    second = upper_half(shape).astype(jnp.int32)
    return [
        [
            jnp.take_along_axis(
                rows[8 * (a // 2) : 8 * (a // 2) + 8], second + (4 * (a % 2) + 2 * h), axis=0
            )
            for h in (0, 1)
        ]
        for a in range(4)
    ]


def triple_product(wide_prolong, operator, near):
    wide = expand(operator)
    out = [None, None]
    for a in range(4):
        inner = fold(wide[a][0] * near[0] + wide[a][1] * near[1])
        for half in range(2):
            term = wide_prolong[a][half] * inner
            out[half] = term if out[half] is None else out[half] + term
    return out


def onehot_rows(targets, count):
    shape = (count, targets.shape[1])
    here = lax.broadcasted_iota(jnp.int32, shape, 0) == jnp.broadcast_to(targets, shape)
    return here.astype(F32).astype(BF16)


def scatter(values, targets, count):
    return add_up(values, onehot_rows(targets, count))


def add_up(values, hot):
    high, low = split(values)
    both = lax.dot_general(
        jnp.concatenate([high, low], axis=0),
        hot,
        (((1,), (1,)), ((), ())),
        preferred_element_type=F32,
    )
    rows = values.shape[0]
    return both[:rows] + both[rows:]


def chunks_of(value):
    return [value[:, at : at + LANES] for at in range(0, value.shape[1], LANES)]


def place():
    sub, slab = lax.axis_index("sub"), lax.axis_index("slab")
    return sub, slab


def neighbours(index, count, even, odd):
    is_even = index % 2 == 0
    if odd is None:
        odd = jnp.zeros_like(even)
    below = jnp.where(is_even, odd, even)
    above = jnp.where(is_even, even, odd)
    below = jnp.where(index > 0, below, jnp.zeros_like(below))
    above = jnp.where(index < count - 1, above, jnp.zeros_like(above))
    return below, above


def swap_halves(below, above, half):
    lane = lax.broadcasted_iota(jnp.int32, below.shape, 1)
    return pltpu.roll(jnp.where(lane < half, above, below), half, 1)


def call(body, outs, *args, scratch=(), flops=0, space=pltpu.VMEM):
    outs = [(out, F32) if isinstance(out[0], int) else out for out in outs]
    cost = pl.CostEstimate(flops=flops, bytes_accessed=0, transcendentals=0) if flops else None
    return pl.pallas_call(
        body,
        out_shape=[jax.ShapeDtypeStruct(shape, dtype) for shape, dtype in outs],
        in_specs=[pl.BlockSpec(memory_space=space)] * len(args),
        out_specs=[pl.BlockSpec(memory_space=pltpu.VMEM)] * len(outs),
        scratch_shapes=list(scratch),
        cost_estimate=cost,
        compiler_params=pltpu.CompilerParams(vmem_limit_bytes=32 * 1024 * 1024),
    )(*args)


def tiles(count, tile, body):
    def step(index, carry):
        body(pl.ds(pl.multiple_of(index * tile, tile), tile))
        return carry

    lax.fori_loop(0, count // tile, step, 0, unroll=True)


def fine_first(handed, slab_moves, *refs):
    count = handed + 3
    raw, refs = refs[:count], refs[count:]
    kept, refs = refs[:handed], refs[handed:]
    operator_raw, prolong, prolong_one, w_ref, first_ref, parity_out, cross_out = refs[:7]
    slab_outs, refs = refs[7 : 7 + slab_moves], refs[7 + slab_moves :]
    prolong_raw, prolong_one_raw, picks, wide_picks, semaphores, slot_semaphores = refs
    source, sends, sends_one = kept[0], kept[1], kept[2]
    targets = [prolong_raw, sends, prolong_one_raw, sends_one, source, *kept[3:]]
    sources = [raw[2], raw[3], raw[4], raw[5], raw[1], *raw[6:]]
    copies = [
        pltpu.make_async_copy(
            value, target if value.ndim > 1 else target.at[0], semaphores.at[at]
        )
        for at, (value, target) in enumerate(zip(sources, targets))
    ]
    slot_copies = [
        pltpu.make_async_copy(raw[0].at[k], operator_raw.at[k], slot_semaphores.at[k])
        for k in range(7)
    ]
    for copy in copies[:5] + slot_copies + copies[5:]:
        copy.start()

    copies[0].wait()
    copies[1].wait()
    for half in range(2):
        at = slice(8 * half, 8 * half + 8)
        prolong[at] = jnp.concatenate([prolong_raw[2 * half], prolong_raw[2 * half + 1]], axis=0)
    wide_table = table_sixteen(chunks_of(prolong[...]))

    def pick_wide(at):
        wide_picks[:, at] = gather_sixteen(wide_table, sends[:, at])

    tiles(sends.shape[1], 512, pick_wide)
    copies[2].wait()
    copies[3].wait()
    for half in range(2):
        at = slice(8 * half, 8 * half + 8)
        prolong_one[at] = jnp.concatenate(
            [prolong_one_raw[2 * half], prolong_one_raw[2 * half + 1]], axis=0
        )
    coarse = gather_sixteen(table_sixteen(chunks_of(prolong_one[...])), sends_one[...])
    sub, slab = place()
    even = sub % 2 == 0
    count = sends.shape[1] // 4
    low_first, high_first = wide_picks[:, 0:count], wide_picks[:, count : 2 * count]
    low_second, high_second = wide_picks[:, 2 * count : 3 * count], wide_picks[:, 3 * count :]
    parity_out[:, 0:count] = jnp.where(even, high_second, low_second)
    cross_out[:, 0:count] = jnp.where(even, low_second, high_second)
    cross_out[:, count + LANES :] = coarse[:, 2 * LANES :]
    for position, out in enumerate(slab_outs):
        up = slab % 2 == position
        out[:, 0:count] = jnp.where(up, high_first, low_first)
        out[:, count + LANES :] = jnp.where(up, coarse[:, LANES : 2 * LANES], coarse[:, 0:LANES])

    sums = [None] * 4
    for k in range(7):
        slot_copies[k].wait()
        for a in range(4):
            value = jnp.abs(operator_raw[k, a])
            sums[a] = value if sums[a] is None else sums[a] + value
    weights = 1.0 + sum_components(jnp.concatenate(sums, axis=0))
    copies[4].wait()
    first = twice(source[...]) / weights
    w_ref[...] = weights
    first_ref[...] = first
    table = table_four(chunks_of(first))
    at = slice(count, count + LANES)
    faces = fine_faces(table, sends, picks)
    parity, cross, slabs = chosen_faces(faces, sub, slab, len(slab_outs))
    parity_out[:, at] = parity
    cross_out[:, at] = cross
    for out, value in zip(slab_outs, slabs):
        out[:, at] = value
    for copy in copies[5:]:
        copy.wait()


def fine_faces(table, sends, picks):
    def pick(at):
        picks[:, at] = gather_four(table, sends[:, at])

    tiles(sends.shape[1], 1024, pick)
    rows = [picks[0:4, at : at + LANES] for at in range(0, sends.shape[1], LANES)]
    each = len(rows) // 4
    return [jnp.concatenate(rows[each * at : each * at + each], axis=0) for at in range(4)]


def chosen_faces(faces, sub, slab, slab_count):
    low_first, high_first, low_second, high_second = faces
    even = sub % 2 == 0
    parity = jnp.where(even, high_second, low_second)
    cross = jnp.where(even, low_second, high_second)
    slabs = [jnp.where(slab % 2 == at, high_first, low_first) for at in range(slab_count)]
    return parity, cross, slabs


def fine_own(operator_raw, prolong, columns, operator, own_near):
    table = table_sixteen(chunks_of(prolong[...]))

    def step(at):
        for k in range(own_near.shape[0] // 16):
            low, high = gather_halves(table, columns[k : k + 1, at], 0)
            own_near[16 * k : 16 * k + 8, at] = low
            own_near[16 * k + 8 : 16 * k + 16, at] = high

    tiles(columns.shape[1], 512, step)
    for k in range(7):
        for half in range(2):
            row = 16 * k + 8 * half
            operator[row : row + 8] = jnp.concatenate(
                [operator_raw[k, 2 * half], operator_raw[k, 2 * half + 1]], axis=0
            )


def fine_ghosts(at, sizes, parity_in, cross_in, slab_ins):
    sub, slab = place()
    slab_values = [ref[:, at] for ref in slab_ins] + [None]
    below, above = neighbours(slab, sizes[1], slab_values[0], slab_values[1])
    left, right = neighbours(sub, sizes[0], parity_in[:, at], cross_in[:, at])
    return [below, above, left, right]


def four_chunks(faces):
    return [twice(face[at : at + 4]) for face in faces for at in range(0, face.shape[0], 4)]


def sixteen_chunks(faces):
    return [chunk for face in faces for chunk in chunks_of(face)]


def apply_tile(table, operator, columns, at):
    total = None
    for k in range(7):
        near = twice(gather_four(table, columns[k : k + 1, at]))
        term = operator[16 * k : 16 * k + 16, at] * near
        total = term if total is None else total + term
    return sum_components(total)


def fine_second(
    sizes, source, operator, columns, sends, w_ref, first_ref, *rest
):
    slab_count = (len(rest) - 6) // 2
    taken, rest = restored(rest[: slab_count + 2], FINE_FIRST), rest[slab_count + 2 :]
    parity_in, cross_in, *slab_ins = taken
    parity_out, cross_out = rest[0], rest[1]
    slab_outs, second_ref, picks = rest[2:-2], rest[-2], rest[-1]
    count = sends.shape[1] // 4
    ghosts = fine_ghosts(
        slice(count, count + LANES), sizes, parity_in, cross_in, slab_ins
    )
    table = table_four(chunks_of(first_ref[...]) + four_chunks(ghosts))

    def step(at):
        residual = twice(source[:, at]) - apply_tile(table, operator, columns, at)
        second_ref[:, at] = first_ref[:, at] + residual / w_ref[:, at]

    tiles(source.shape[1], source.shape[1], step)
    faces = fine_faces(table_four(chunks_of(second_ref[...])), sends, picks)
    sub, slab = place()
    parity, cross, slabs = chosen_faces(faces, sub, slab, len(slab_outs))
    parity_out[:, 0:LANES] = parity
    parity_out[:, LANES:] = cross_in[:, count + LANES :]
    cross_out[...] = cross
    for out, value in zip(slab_outs, slabs):
        out[...] = value


def coarsen(tables, operator, prolong, columns, slots, aggregates, sums, count, own_near=None):
    tile = 256
    whole = jnp.concatenate(tables, axis=0)
    known = 0 if own_near is None else own_near.shape[0] // 16

    def step(at):
        wide_prolong = expand(prolong[:, at])
        totals = [[jnp.zeros((8, tile), F32) for _ in range(2)] for _ in range(7)]
        for k in range(7):
            column = columns[k : k + 1, at]
            if k < known:
                row = 16 * k
                own = [own_near[row : row + 8, at], own_near[row + 8 : row + 16, at]]
                near = gather_halves(tables[1], column, tables[0].shape[0] // 16, own)
            else:
                near = gather_halves(whole, column, 0)
            blocks = triple_product(wide_prolong, operator[16 * k : 16 * k + 16, at], near)
            slot = jnp.broadcast_to(slots[k : k + 1, at], (8, tile))
            for s in range(7):
                here = slot == s
                for half in range(2):
                    totals[s][half] = totals[s][half] + jnp.where(here, blocks[half], 0.0)
        for s in range(7):
            for half in range(2):
                row = 16 * s + 8 * half
                sums[row : row + 8, at] = totals[s][half]

    tiles(columns.shape[1], tile, step)
    return scatter(sums[...], aggregates[...], count)


def fine_coarsen(
    sizes,
    operator,
    prolong,
    columns,
    slots,
    aggregates,
    own_near,
    second_ref,
    parity_old,
    cross_old,
    *rest,
):
    slab_old, (out, sums) = rest[:-2], rest[-2:]
    count = parity_old.shape[1] - LANES
    ghosts = fine_ghosts(slice(0, count), sizes, parity_old, cross_old, slab_old)
    tables = [table_sixteen(chunks_of(prolong[...])), table_sixteen(sixteen_chunks(ghosts))]
    out[...] = coarsen(
        tables, operator, prolong, columns, slots, aggregates, sums, out.shape[1], own_near
    )


def fine_restrict(
    sizes,
    source,
    operator,
    prolong,
    columns,
    aggregates,
    second_ref,
    operator_own,
    *rest,
):
    parity_in, cross_in, *slab_ins = restored(rest[:-2], FINE_SECOND)
    out, lifted = rest[-2:]
    ghosts = fine_ghosts(slice(0, LANES), sizes, parity_in, cross_in, slab_ins)
    table = table_four(chunks_of(second_ref[...]) + four_chunks(ghosts))

    def step(at):
        residual = twice(source[:, at]) - apply_tile(table, operator, columns, at)
        lifted[:, at] = lift(prolong[:, at], residual)

    tiles(source.shape[1], source.shape[1], step)
    out[0:112] = operator_own[...]
    out[112:120] = scatter(lifted[...], aggregates[...], out.shape[1])


def pair_faces(picks, sub, slab, outs):
    for position, out in enumerate(outs):
        face = jnp.where(
            slab % 2 == position, picks[:, LANES : 2 * LANES], picks[:, 0:LANES]
        )
        out[...] = jnp.where(sub % 2 == 0, face, picks[:, 2 * LANES :])


def pair_first(own, other, sends, operator, source, weights, first, *outs):
    sub, slab = place()
    even = sub % 2 == 0
    half = own.shape[1]
    lower = jnp.where(even, own[...], other[...])
    upper = jnp.where(even, other[...], own[...])
    operator[:, 0:half] = lower[0:112]
    operator[:, half:] = upper[0:112]
    source[:, 0:half] = lower[112:120]
    source[:, half:] = upper[112:120]
    weights[...] = row_weights(lambda k: operator[16 * k : 16 * k + 16])
    first[...] = source[...] / weights[...]
    picks = gather_four(table_four(chunks_of(first[...])), sends[...])
    pair_faces(picks, sub, slab, outs)


def pair_ghosts(sizes, mine, other):
    sub, slab = place()
    even = sub % 2 == 0
    mine, other = [mine[0:8], mine[8:16]], [other[0:8], other[8:16]]
    along_slab = [jnp.where(even, mine[at], other[at]) for at in range(2)]
    along_sub = [jnp.where(even, other[at], mine[at]) for at in range(2)]
    below, above = neighbours(
        slab, sizes[1], along_slab[0], along_slab[1] if sizes[1] > 2 else None
    )
    left, right = neighbours(sub // 2, sizes[0] // 2, along_sub[0], along_sub[1])
    return [below, above, swap_halves(left, right, LANES // 2)]


def pair_second(
    sizes, operator, source, weights, first, columns, sends, mine, other, second_ref, *outs
):
    table = table_four(chunks_of(first[...]) + pair_ghosts(sizes, mine, other))

    def step(at):
        residual = source[:, at] - apply_tile(table, operator, columns, at)
        second_ref[:, at] = first[:, at] + residual / weights[:, at]

    tiles(source.shape[1], 512, step)
    sub, slab = place()
    picks = gather_four(table_four(chunks_of(second_ref[...])), sends[...])
    pair_faces(picks, sub, slab, outs)


def pair_coarsen(
    sizes,
    operator,
    prolong,
    columns,
    slots,
    aggregates,
    sends,
    second_fine,
    second_ref,
    parity_old,
    cross_old,
    forwarded,
    *rest,
):
    slab_old, rest = rest[:-7], rest[-7:]
    operator_two, weights_two, face_weights, hot_out, smoothed, smoothed_one, sums = rest
    sub, slab = place()
    even = sub % 2 == 0
    half = smoothed_one.shape[1]
    smoothed[...] = second_fine[0:4]
    smoothed_one[...] = jnp.where(even, second_ref[0:4, 0:half], second_ref[0:4, half:])
    after = parity_old.shape[1]
    values = [ref[:, after:] for ref in slab_old] + [None]
    below, above = neighbours(slab, sizes[1], values[0], values[1])
    mine = cross_old[:, after:]
    partners = forwarded[:, LANES:]
    group = sub // 2
    left = jnp.where(even, mine, partners)
    right = jnp.where(even, partners, mine)
    left = jnp.where(group > 0, left, jnp.zeros_like(left))
    right = jnp.where(group < sizes[0] // 2 - 1, right, jnp.zeros_like(right))
    ghosts = [below, above, swap_halves(left, right, LANES // 2)]
    tables = [table_sixteen(chunks_of(prolong[...])), table_sixteen(ghosts)]
    operator_two[...] = coarsen(
        tables, operator, prolong, columns, slots, aggregates, sums, LANES
    )
    weights = row_weights(lambda k: operator_two[16 * k : 16 * k + 16])
    weights_two[...] = weights
    filler = jnp.zeros((1, -sends.shape[1] % LANES), jnp.int32)
    rows = jnp.concatenate([sends[...], filler], axis=1) - group % 2 * (LANES // 2)
    face_weights[...] = gather_four(table_four([weights]), rows & (LANES - 1))
    hot = onehot_rows(aggregates[...], LANES)
    hot_out[0:LANES] = hot
    hot_out[LANES:] = lax.dot_general(
        onehot(rows)[0:LANES], hot, (((0,), (0,)), ((), ())), preferred_element_type=F32
    ).astype(BF16)


def pair_restrict(
    sizes,
    operator,
    source,
    second_ref,
    prolong,
    columns,
    weights_two,
    face_weights,
    hot,
    *rest,
):
    mine, other, *rest = rest
    source_two, first_two, whole_out = rest[:3]
    slab_outs, lifted = rest[3:-1], rest[-1]
    sub, slab = place()
    table = table_four(chunks_of(second_ref[...]) + pair_ghosts(sizes, mine, other))

    def step(at):
        residual = source[:, at] - apply_tile(table, operator, columns, at)
        lifted[:, at] = lift(prolong[:, at], residual)

    tiles(source.shape[1], 512, step)
    totals = add_up(lifted[...], hot[...])
    total = totals[:, 0:LANES]
    source_two[...] = total
    first = total / weights_two[...]
    first_two[...] = first
    half = LANES // 2
    lane = lax.broadcasted_iota(jnp.int32, first.shape, 1)
    picks = totals[:, LANES:] / face_weights[...]
    faces = picks[:, 0:LANES]
    seconds = pltpu.roll(picks[:, LANES:], half, 1)

    def sent(value):
        return jnp.where(lane < half, value, seconds)

    slab_even = slab % 2 == 0
    for position, out in enumerate(slab_outs):
        up = slab_even if position == 0 else jnp.logical_not(slab_even)
        out[...] = sent(jnp.where(up, pltpu.roll(faces, half, 1), faces))
    whole_out[...] = jnp.where(sub % 2 == 0, sent(first), slab_outs[0][...])


def group_apply(sizes, operator, first_two, columns, *rest):
    received, out = restored(rest[:-1], GROUP), rest[-1]
    sub, slab = place()
    group, pair = sub // 4, sub // 2 % 2
    even = sub % 2 == 0
    half = LANES // 2
    lane = lax.broadcasted_iota(jnp.int32, (8, LANES), 1)

    def left_part(value):
        return jnp.where(lane < half, value, 0.0)

    mine, other = left_part(first_two[...]), left_part(received[0][...])
    first = jnp.where(
        pair == 0, mine + pltpu.roll(other, half, 1), other + pltpu.roll(mine, half, 1)
    )
    first = jnp.where(even, first, jnp.zeros_like(first))

    slab_even = jnp.where(even, received[1][...], received[0][...])
    slab_odd = received[4][...] if len(received) > 4 else None
    below, above = neighbours(slab, sizes[1], slab_even, slab_odd)
    firsts = left_part(below) + pltpu.roll(left_part(above), half, 1)

    group_even = jnp.where(even, received[2][...], received[1][...])
    group_odd = jnp.where(even, received[3][...], received[2][...])
    left, right = neighbours(group, sizes[0] // 4, group_even, group_odd)
    width = GX // 4 * (GZ // 4)
    left = pltpu.roll(left, LANES - half - width, 1)
    right = pltpu.roll(right, LANES - half + width, 1)
    seconds = jnp.where(lane < width, left, jnp.where(lane < 2 * width, right, 0.0))

    table = table_four([first, firsts, seconds])
    mine = jnp.where(pair == 0, columns[...], pltpu.roll(columns[...], half, 1))
    total = None
    for k in range(7):
        near = twice(gather_four(table, mine[k : k + 1]))
        term = operator[16 * k : 16 * k + 16] * near
        total = term if total is None else total + term
    out[...] = sum_components(total)


def group_second(source, weights, first_two, own, other, out):
    sub, slab = place()
    residual = source[...] - (own[...] + other[...])
    second = first_two[...] + residual / weights[...]
    share = out.shape[1]
    out[...] = jnp.where(sub % 2 == 0, second[0:4, 0:share], second[0:4, share : 2 * share])


def other_core(sub, slab):
    return sub ^ 1, slab


def swap_by_core(value, even_mate, odd_mate, even_spare=None, odd_spare=None):
    subs, slabs = lax.axis_size("sub"), lax.axis_size("slab")
    route = []
    for sub in range(subs):
        for slab in range(slabs):
            even = sub % 2 == 0
            target = (even_mate if even else odd_mate)(sub, slab)
            if not (0 <= target[0] < subs and 0 <= target[1] < slabs):
                spare = even_spare if even else odd_spare
                target = (sub ^ 2, slab) if spare is None else spare(sub, slab)
            route.append((sub * slabs + slab, target[0] * slabs + target[1]))
    return lax.ppermute(value, ("sub", "slab"), route)


def odd_mate_of(index):
    return ((index - 1) ^ 1) + 1


def along_sub(group, odd, flip):
    def mate(sub, slab):
        block = odd_mate_of(sub // group) if odd else sub // group ^ 1
        return block * group + (sub % group ^ flip), slab

    return mate


def along_slab(odd, flip):
    return lambda sub, slab: (sub ^ flip, odd_mate_of(slab) if odd else slab ^ 1)


def pair_exchange(first, second, beside=lambda: ()):
    def idle(sub, slab):
        return sub ^ 2, slab

    def beside_slab(sub, slab):
        return sub, slab ^ 1

    last = along_sub(2, True, 0)
    received = [swap_by_core(first, along_slab(False, 0), along_sub(2, False, 0))]
    if lax.axis_size("slab") > 2:
        received.append(swap_by_core(second, along_slab(True, 0), last, None, beside_slab))
    else:
        received.append(swap_by_core(second, idle, last, None, beside_slab))
    mine = jnp.concatenate(received, axis=0)
    mine, results = lax.optimization_barrier((mine, beside()))
    return mine, sub_pairing(mine, 1, False), results


def group_exchange(whole, slab_values):
    def pair(sub, slab):
        return sub ^ 2, slab

    def idle(sub, slab):
        inside = 0 <= odd_mate_of(sub // 4) < lax.axis_size("sub") // 4
        return sub ^ (2 if inside else 1), slab

    first = slab_values[0]
    received = [
        swap_by_core(whole, pair, along_slab(False, 2)),
        swap_by_core(first, along_slab(False, 0), along_sub(4, False, 2)),
        swap_by_core(first, along_sub(4, False, 0), along_sub(4, True, 2)),
        swap_by_core(first, along_sub(4, True, 0), idle, other_core, other_core),
    ]
    for value in slab_values[1:]:
        received.append(swap_by_core(value, along_slab(True, 0), along_slab(True, 2)))
    return received


def sub_pairing(value, group, odd):
    subs, slabs = lax.axis_size("sub"), lax.axis_size("slab")
    route = []
    for sub in range(subs):
        block = sub // group
        mate = ((block - 1) ^ 1) + 1 if odd else block ^ 1
        for slab in range(slabs):
            target = (mate * group + sub % group, slab)
            if not 0 <= mate < subs // group:
                target = (sub ^ group // 2, slab) if group > 1 else (sub, slab ^ 1)
            route.append((sub * slabs + slab, target[0] * slabs + target[1]))
    return lax.ppermute(value, ("sub", "slab"), route)


def slab_pairing(value, odd):
    subs, slabs = lax.axis_size("sub"), lax.axis_size("slab")
    route = []
    for sub in range(subs):
        for slab in range(slabs):
            mate = ((slab - 1) ^ 1) + 1 if odd else slab ^ 1
            target = (sub, mate) if 0 <= mate < slabs else (sub ^ 1, slab)
            route.append((sub * slabs + slab, target[0] * slabs + target[1]))
    return lax.ppermute(value, ("sub", "slab"), route)


def slab_pairings(values):
    return [slab_pairing(value, position == 1) for position, value in enumerate(values)]


def on_device(
    source,
    operator,
    prolong,
    columns,
    slots,
    aggregates,
    sends,
    prolong_one,
    columns_one,
    slots_one,
    aggregates_one,
    sends_one,
    columns_two,
    sends_two,
):
    sizes = (lax.axis_size("sub"), lax.axis_size("slab"))
    slab_moves = 1 if sizes[1] == 2 else 2
    rows = source.shape[1]
    rows_one = rows // 8
    pair_rows_one = 2 * rows_one
    count = 2 * GY * GZ
    kept = [
        source,
        sends,
        sends_one,
        columns,
        slots,
        aggregates,
        columns_one,
        slots_one,
        aggregates_one,
        columns_two,
        sends_two,
    ]
    raw = [operator, kept[0], prolong, kept[1], prolong_one, kept[2], *kept[3:]]
    handed = len(kept)
    out = call(
        functools.partial(fine_first, handed, slab_moves),
        [((1, value.shape[0]) if value.ndim == 1 else value.shape, value.dtype) for value in kept]
        + [operator.shape, (16, rows), (16, pair_rows_one)]
        + [(8, rows), (8, rows), (16, count + LANES), (16, count + 2 * LANES)]
        + [(16, count + 2 * LANES)] * slab_moves,
        *[pltpu.with_memory_space_constraint(value, pltpu.HBM) for value in raw],
        scratch=[
            pltpu.VMEM(prolong.shape, F32),
            pltpu.VMEM(prolong_one.shape, F32),
            pltpu.VMEM((8, rows), F32),
            pltpu.VMEM((16, rows), F32),
            pltpu.SemaphoreType.DMA((len(raw) - 1,)),
            pltpu.SemaphoreType.DMA((7,)),
        ],
        space=pltpu.HBM,
    )
    source, sends, sends_one, columns, slots, aggregates = out[:6]
    columns_one, slots_one, aggregates_one, columns_two, sends_two = out[6:11]
    operator_raw, prolong, prolong_one, weights, first, even, odd, *slabs = out[11:]
    even_old = sub_pairing(even, 1, False)
    odd_old = sub_pairing(odd, 1, True)
    slabs_old = slab_pairings(slabs)

    operator, own_near = call(
        fine_own,
        [(112, rows), (16 * OWN_SLOTS, rows)],
        operator_raw,
        prolong,
        columns,
        flops=10**9,
    )
    even, odd, *rest = call(
        functools.partial(fine_second, sizes),
        [(16, 2 * LANES), (16, LANES)]
        + [(16, LANES)] * slab_moves
        + [(8, rows)],
        source,
        operator,
        columns,
        sends,
        weights,
        first,
        *ordered([even_old, odd_old, *slabs_old], FINE_FIRST),
        scratch=[pltpu.VMEM((8, sends.shape[1]), F32)],
    )
    slabs, second = rest[:-1], rest[-1]
    forwarded = sub_pairing(even, 1, False)
    odd_in = sub_pairing(odd, 1, True)
    slabs_in = slab_pairings(slabs)

    (operator_own,) = call(
        functools.partial(fine_coarsen, sizes),
        [(112, rows_one)],
        operator,
        prolong,
        columns,
        slots,
        aggregates,
        own_near,
        second,
        even_old,
        odd_old,
        *slabs_old,
        scratch=[pltpu.VMEM((112, rows), F32)],
        flops=4 * 10**9,
    )
    (own,) = call(
        functools.partial(fine_restrict, sizes),
        [(120, rows_one)],
        source,
        operator,
        prolong,
        columns,
        aggregates,
        second,
        operator_own,
        *ordered([forwarded, odd_in, *slabs_in], FINE_SECOND),
        scratch=[pltpu.VMEM((8, rows), F32)],
    )
    other = sub_pairing(own, 1, False)

    faces = [(8, LANES)] * (1 + slab_moves)
    pair_sent = [(8, LANES)] * 2
    operator_one, source_one, weights_one, first_one, *sent = call(
        pair_first,
        [(112, pair_rows_one)] + [(8, pair_rows_one)] * 3 + pair_sent,
        own,
        other,
        sends_one,
    )
    mine, other, _ = pair_exchange(*sent)

    second_one, *sent = call(
        functools.partial(pair_second, sizes),
        [(8, pair_rows_one)] + pair_sent,
        operator_one,
        source_one,
        weights_one,
        first_one,
        columns_one,
        sends_one,
        mine,
        other,
    )
    def coarse_operator():
        return call(
            functools.partial(pair_coarsen, sizes),
            [(112, LANES), (8, LANES), (8, 2 * LANES), ((3 * LANES, pair_rows_one), BF16)]
            + [(4, rows), (4, rows_one)],
            operator_one,
            prolong_one,
            columns_one,
            slots_one,
            aggregates_one,
            sends_two,
            second,
            second_one,
            even_old,
            odd_old,
            forwarded,
            *slabs_old,
            scratch=[pltpu.VMEM((112, pair_rows_one), F32)],
            flops=10**9,
        )

    mine, other, outs = pair_exchange(*sent, beside=coarse_operator)
    operator_two, weights_two, face_weights, hot, smoothed, smoothed_one = outs

    source_two, first_two, whole, *slabs = call(
        functools.partial(pair_restrict, sizes),
        [(8, LANES), (8, LANES)] + faces,
        operator_one,
        source_one,
        second_one,
        prolong_one,
        columns_one,
        weights_two,
        face_weights,
        hot,
        mine,
        other,
        scratch=[pltpu.VMEM((8, pair_rows_one), F32)],
    )
    received = group_exchange(whole, slabs)
    (applied,) = call(
        functools.partial(group_apply, sizes),
        [(8, LANES)],
        operator_two,
        first_two,
        columns_two,
        *ordered(received, GROUP),
    )
    applied_other = sub_pairing(applied, 1, False)
    (smoothed_two,) = call(
        group_second,
        [(4, rows_one // 8)],
        source_two,
        weights_two,
        first_two,
        applied,
        applied_other,
    )
    return (smoothed, smoothed_one, smoothed_two)


def solution(mesh):
    placed = (
        P(None, ("sub", "slab")),
        P(None, None, None, ("sub", "slab")),
        P(None, None, ("sub", "slab")),
        P(None, ("sub", "slab")),
        P(None, ("sub", "slab")),
        P(("sub", "slab")),
        P(("sub", "slab")),
        P(None, None, ("sub", "slab")),
        P(None, ("sub", "slab")),
        P(None, ("sub", "slab")),
        P(("sub", "slab")),
        P(("sub", "slab")),
        P(None, ("sub", "slab")),
        P(("sub", "slab")),
    )
    return jax.shard_map(
        on_device,
        mesh=mesh,
        in_specs=placed,
        out_specs=(P(None, ("sub", "slab")), P(None, ("sub", "slab")), P(None, ("sub", "slab"))),
        check_vma=False,
    )
```
